512 devices in a mesh: dp: 64 (over z, y_hi, core), tensor: 8 (over y_lo, x).
Axes of the slice: x: 4, y: 8 (y_hi: 4, y_lo: 2; y = y_hi * 2 + y_lo), z: 8, core: 2. Of those that a mesh axis runs over, the one named last changes fastest.
Arguments:
- tokens: bfloat16 [24576, 4096], P('dp'), may hold values from -6 to 6
- doc_lengths: int32 [128], P('dp'), may hold values from 1 to 192, as said below
- gate_weight: bfloat16 [4096, 7168], P('dp', 'tensor'), may hold values from -0.09375 to 0.09375
- up_weight: bfloat16 [4096, 7168], P('dp', 'tensor'), may hold values from -0.09375 to 0.09375
- hidden_grad: bfloat16 [24576, 7168], P('dp', 'tensor'), may hold values from -6 to 6
- in_projector: bfloat16 [64, 4096], replicated, may hold values from -0.09375 to 0.09375
- gate_projector: bfloat16 [64, 7168], P(None, 'tensor'), may hold values from -0.0625 to 0.0625
- up_projector: bfloat16 [64, 7168], P(None, 'tensor'), may hold values from -0.0625 to 0.0625
Outputs:
- gate_features: float32 [128, 64, 64], P('dp', None, 'tensor')
- up_features: float32 [128, 64, 64], P('dp', None, 'tensor')
The draws below stay inside these ranges and needn't reach their ends.
Inputs may be any that keep to these rules, and one draw needn't show every extreme that they name: `doc_lengths`: at least one document in every draw has all 192 slots used.
All inputs are finite; a program needn't handle non-finite values.
Results may differ from the reference program's by a relative error of at most 0.013.
Values may be sent and summed in bfloat16 or wider, within the bound.
A program may use at most 64 MiB of HBM per device.

```python
import jax
import jax.numpy as jnp
from jax import lax

D = 4096
FF = 7168
R = 64
DOC_LEN = 192
DOCS = 128
TOKENS = 24576


def draw_doc_lengths(key, part):
    key = jax.random.fold_in(key, 5)
    first, second = jax.random.split(key)
    lengths = jax.random.randint(first, (DOCS,), 1, DOC_LEN + 1)
    where = jax.random.randint(second, (), 0, DOCS)
    return jnp.where(jnp.arange(DOCS) == where, DOC_LEN, lengths).astype(jnp.int32)


def level_of(key, dims, cuts, low, largest):
    gain, own = 1.0, jax.random.fold_in(key, 6)
    for dim, blocks in cuts:
        steps = jnp.exp(jax.random.uniform(jax.random.fold_in(own, dim), (blocks,), jnp.float32, low / len(cuts), largest / len(cuts)))
        gain = gain * jnp.repeat(steps, dims[dim] // blocks).reshape([-1 if axis == dim else 1 for axis in range(len(dims))])
    return gain


def normal_values(own_key, extent, deviation, bound, shards=(), held_as=jnp.bfloat16):
    drawn = jax.random.normal(own_key, extent, jnp.float32) * deviation
    if len(shards) > 0:
        drawn = level_of(own_key, extent, shards, -0.22, 0.18) * drawn
    return jnp.clip(drawn, min=-bound, max=bound).astype(held_as)


def setup_inputs(seed: int = 0) -> dict:
    key_list = jax.random.split(jax.random.key(seed), 9)
    tokens = normal_values(key_list[0], (TOKENS, D), 1.0, 6.0, ((0, 64),))
    doc_lengths = draw_doc_lengths(jax.random.fold_in(key_list[8], 71), 0)
    gate_weight = normal_values(key_list[2], (D, FF), D ** -0.5, 0.09375, ((0, 64), (1, 8)))
    up_weight = normal_values(key_list[3], (D, FF), D ** -0.5, 0.09375, ((0, 64), (1, 8)))
    hidden_grad = normal_values(key_list[4], (TOKENS, FF), 1.0, 6.0, ((0, 64), (1, 8)))
    in_projector = normal_values(key_list[5], (R, D), D ** -0.5, 0.09375)
    gate_projector = normal_values(key_list[6], (R, FF), FF ** -0.5, 0.0625, ((1, 8),))
    up_projector = normal_values(key_list[7], (R, FF), FF ** -0.5, 0.0625, ((1, 8),))
    return {"tokens": tokens, "doc_lengths": doc_lengths, "gate_weight": gate_weight, "up_weight": up_weight, "hidden_grad": hidden_grad, "in_projector": in_projector, "gate_projector": gate_projector, "up_projector": up_projector}


def contract_last(left, right):
    return lax.dot_general(left, right, (((1,), (1,)), ((), ())), preferred_element_type=jnp.float32)


def per_document(inputs, side):
    left = inputs.astype(jnp.float32).reshape(DOCS, DOC_LEN, R)
    right = side.astype(jnp.float32).reshape(DOCS, DOC_LEN, R)
    return 0.0625 * jnp.einsum("ntr,nts->nrs", left, right, precision=lax.Precision.HIGHEST)


def reference(tokens, doc_lengths, gate_weight, up_weight, hidden_grad, in_projector, gate_projector, up_projector):
    gate = jnp.dot(tokens, gate_weight, preferred_element_type=jnp.float32)
    up = jnp.dot(tokens, up_weight, preferred_element_type=jnp.float32)
    sig = jax.nn.sigmoid(gate)
    cotangent = hidden_grad.astype(jnp.float32)
    grad_gate = (cotangent * up * sig * (1.0 + gate * (1.0 - sig))).astype(jnp.bfloat16)
    grad_up = (cotangent * gate * sig).astype(jnp.bfloat16)
    position = jnp.arange(TOKENS, dtype=jnp.int32)
    owner = position // DOC_LEN
    within = position % DOC_LEN
    mask = (within < doc_lengths[owner]).astype(jnp.bfloat16)
    inputs = contract_last(tokens, in_projector).astype(jnp.bfloat16) * mask[:, None]
    gate_side = contract_last(grad_gate, gate_projector).astype(jnp.bfloat16)
    up_side = contract_last(grad_up, up_projector).astype(jnp.bfloat16)
    return per_document(inputs, gate_side), per_document(inputs, up_side)
```

```python
import jax
import jax.numpy as jnp
from jax import lax
from jax.experimental import pallas as pl
from jax.experimental.pallas import tpu as pltpu
from jax.sharding import PartitionSpec as P

MESH = pl.DeviceIdType.MESH
DOC_LEN = 192
ROWS = 384
D = 4096
COLS = 896
RANK = 64
ALIGNED = 384
HALF = 512
ZS, YS = 8, 4
BLOCK = D // ZS
SHARD = 64
PIECE = 16
SUBS = 3
ORDER = (0, 1, 3, 2)
LAST_RIGHT, LAST_LEFT = (0, 3), (1, 2)


def contract_last(left, right):
    return lax.dot_general(
        left, right, (((1,), (1,)), ((), ())), preferred_element_type=jnp.float32
    )


def kernel(
    len_ref, tok_hbm, gw_hbm, uw_hbm, hg_hbm, inp_hbm, gp_hbm, up_hbm,
    og_ref, ou_ref,
    tok, tokp, gw, uw, other, w5, hgo, hgp, inp, gp, up,
    acc, grads, proj, parts, arrived, in_t,
    loc_sem, w1_s, w1_r, zr_s, zr_r, zl_s, zl_r, sib_s, sib_r,
    t1_s, t1_r, t2_s, t2_r, xr_s, xr_r, xl_s, xl_r, hg_s, hg_r, rs_s, rs_r,
):
    dp, t = lax.axis_index("dp"), lax.axis_index("tensor")
    z, yh, c = dp // 8, (dp // 2) % YS, dp % 2
    yl, x = t // 4, t % 4
    p = yh % 2
    yhp = yh + 1 - 2 * p

    def at(z_, yh_, c_, yl_, x_):
        return (z_ * 8 + yh_ * 2 + c_, yl_ * 4 + x_)

    z_right, z_left = at((z + 1) % ZS, yh, c, yl, x), at((z + ZS - 1) % ZS, yh, c, yl, x)
    sibling = at(z, yh, 1 - c, yl, x)
    pair = at(z, yhp, c, yl, x)
    y_sib = at(z, yh, c, 1 - yl, x)
    x_right, x_left = at(z, yh, c, yl, (x + 1) % 4), at(z, yh, c, yl, (x + 3) % 4)
    pair_dp = pair[0]

    off = pl.multiple_of(p * HALF, 128)
    local = [
        pltpu.make_async_copy(gw_hbm, gw, loc_sem.at[0]),
        pltpu.make_async_copy(uw_hbm, uw, loc_sem.at[1]),
        pltpu.make_async_copy(tok_hbm, tok, loc_sem.at[2]),
        pltpu.make_async_copy(hg_hbm.at[:, pl.ds(off, ALIGNED)], hgo.at[:, pl.ds(0, ALIGNED)], loc_sem.at[3]),
        pltpu.make_async_copy(hg_hbm.at[:, pl.ds(ALIGNED, 128)], hgo.at[:, pl.ds(ALIGNED, 128)], loc_sem.at[4]),
        pltpu.make_async_copy(inp_hbm, inp, loc_sem.at[5]),
        pltpu.make_async_copy(gp_hbm.at[:, pl.ds(off, ALIGNED)], gp.at[:, pl.ds(0, ALIGNED)], loc_sem.at[6]),
        pltpu.make_async_copy(gp_hbm.at[:, pl.ds(ALIGNED, 128)], gp.at[:, pl.ds(ALIGNED, 128)], loc_sem.at[7]),
        pltpu.make_async_copy(up_hbm.at[:, pl.ds(off, ALIGNED)], up.at[:, pl.ds(0, ALIGNED)], loc_sem.at[8]),
        pltpu.make_async_copy(up_hbm.at[:, pl.ds(ALIGNED, 128)], up.at[:, pl.ds(ALIGNED, 128)], loc_sem.at[9]),
    ]
    for copy in local:
        copy.start()

    barrier = pltpu.get_barrier_semaphore()
    greeted = [z_right, z_left, sibling, at(z, (yh + 2) % YS, c, yl, x), at(z, (yhp + 2) % YS, c, yl, x)]
    for who in greeted:
        pl.semaphore_signal(barrier, inc=1, device_id=who, device_id_type=MESH)
    for k in range(1, 8):
        pl.semaphore_signal(barrier, inc=1, device_id=(dp, (t + k) % 8), device_id_type=MESH)
    for k in range(8):
        pl.semaphore_signal(barrier, inc=1, device_id=(pair_dp, (t + k) % 8), device_id_type=MESH)

    local[0].wait()
    local[1].wait()
    lane = lax.broadcasted_iota(jnp.int32, (SHARD, 128), 1)
    g3 = gw[:, ALIGNED:HALF].astype(jnp.float32)
    u3 = pltpu.roll(uw[:, ALIGNED:HALF].astype(jnp.float32), 64, 1)
    mid0 = jnp.where(lane < 64, g3, u3).astype(jnp.bfloat16)
    mid1 = jnp.where(lane < 64, u3, g3).astype(jnp.bfloat16)

    def pack(even):
        lo = jnp.concatenate([gw[:, :ALIGNED], mid0, uw[:, :ALIGNED]], axis=1)
        hi = jnp.concatenate([gw[:, HALF:], mid1, uw[:, HALF:]], axis=1)
        return jnp.where(even, lo, hi)

    w5[z, yh, c] = pack(p == 0)
    other[...] = pack(p == 1)

    pl.semaphore_wait(barrier, len(greeted) + 15)

    started = []

    def send(src, dst, ss, rs, who):
        copy = pltpu.make_async_remote_copy(
            src_ref=src, dst_ref=dst, send_sem=ss, recv_sem=rs, device_id=who, device_id_type=MESH
        )
        copy.start()
        started.append(copy)

    def landed(dst, ss, rs):
        pltpu.make_async_remote_copy(
            src_ref=dst, dst_ref=dst, send_sem=ss, recv_sem=rs, device_id=sibling, device_id_type=MESH
        ).wait_recv()

    def chunk(dz, k):
        return w5.at[(z + dz + 2 * ZS) % ZS, (yh + k) % YS, c]

    def z_send_right(s, k):
        i = (s - 1) * 4 + k
        ref = chunk(1 - s, k)
        send(ref, ref, zr_s.at[i], zr_r.at[i], z_right)

    def z_send_left(s, k):
        i = (s - 1) * 4 + k
        ref = chunk(s - 1, k)
        send(ref, ref, zl_s.at[i], zl_r.at[i], z_left)

    def pass_on(s, k):
        if s < 4 or k in LAST_RIGHT:
            z_send_right(s, k)
        if s < 4 or k in LAST_LEFT:
            z_send_left(s, k)

    def z_wait(s, k):
        i = (s - 1) * 4 + k
        if s < 4 or k in LAST_RIGHT:
            landed(chunk(-s, k), zr_s.at[i], zr_r.at[i])
        if s < 4 or k in LAST_LEFT:
            landed(chunk(s, k), zl_s.at[i], zl_r.at[i])
        if s < 4:
            pass_on(s + 1, k)

    def sib_send(i, dz, k=None):
        ref = w5.at[(z + dz + ZS) % ZS, :, c] if k is None else chunk(dz, k)
        send(ref, ref, sib_s.at[i], sib_r.at[i], sibling)

    def sib_wait(i, dz, k=None):
        zz = (z + dz + ZS) % ZS
        ref = w5.at[zz, :, 1 - c] if k is None else w5.at[zz, (yh + k) % YS, 1 - c]
        landed(ref, sib_s.at[i], sib_r.at[i])

    def piece(xx, yy, i):
        start = 96 * ((x + xx + 4) % 4) + 48 * yy + PIECE * i
        return pl.ds(pl.multiple_of(start, PIECE), PIECE)

    def t1_send(i):
        rows = piece(0, yl, i)
        send(tok_hbm.at[rows], tokp.at[rows], t1_s.at[i], t1_r.at[i], pair)

    def x_sends(i, yy, n):
        ref = tokp.at[piece(0, yy, i)]
        send(ref, ref, xr_s.at[n], xr_r.at[n], x_right)
        send(ref, ref, xl_s.at[n], xl_r.at[n], x_left)

    def t1_wait(i):
        ref = tokp.at[piece(0, yl, i)]
        landed(ref, t1_s.at[i], t1_r.at[i])
        send(ref, ref, t2_s.at[i], t2_r.at[i], y_sib)
        x_sends(i, yl, i)

    def t2_wait(i):
        landed(tokp.at[piece(0, 1 - yl, i)], t2_s.at[i], t2_r.at[i])
        x_sends(i, 1 - yl, SUBS + i)

    def x_wait(i, near):
        n, yy = (i, yl) if near else (SUBS + i, 1 - yl)
        ref_l, ref_r = tokp.at[piece(-1, yy, i)], tokp.at[piece(1, yy, i)]
        landed(ref_l, xr_s.at[n], xr_r.at[n])
        landed(ref_r, xl_s.at[n], xl_r.at[n])
        m = 2 * SUBS + i
        if near:
            send(ref_l, ref_l, xr_s.at[m], xr_r.at[m], x_right)
        else:
            send(ref_r, ref_r, xl_s.at[m], xl_r.at[m], x_left)

    def far_wait(i):
        m = 2 * SUBS + i
        landed(tokp.at[piece(-2, yl, i)], xr_s.at[m], xr_r.at[m])
        landed(tokp.at[piece(2, 1 - yl, i)], xl_s.at[m], xl_r.at[m])

    def product(held, row, zz, first=False):
        columns = pl.ds(pl.multiple_of(zz * BLOCK, BLOCK), BLOCK)
        term = jnp.dot(
            held[:, columns], w5[zz].reshape(BLOCK, COLS), preferred_element_type=jnp.float32
        )
        if first:
            acc[row : row + ROWS, :] = term
        else:
            acc[row : row + ROWS, :] += term

    def own(dz, first=False):
        product(tok, 0, (z + dz + ZS) % ZS, first)

    def paired(dz, first=False):
        product(tokp, ROWS, (z + dz + ZS) % ZS, first)

    pass_on(1, 0)
    mine = w5.at[z, yh, c]
    for d in (1, 3):
        send(other, mine, w1_s.at[d - 1], w1_r.at[3 - d], at(z, (yh + d) % YS, c, yl, x))
    send(mine, mine, w1_s.at[1], w1_r.at[1], at(z, (yh + 2) % YS, c, yl, x))
    for i in range(SUBS):
        t1_send(i)

    def w1_wait(k):
        landed(chunk(0, k), w1_s.at[k - 1], w1_r.at[k - 1])
        pass_on(1, k)

    for copy in local[3:]:
        copy.wait()
    side_lane = lax.broadcasted_iota(jnp.int32, (RANK, HALF), 1)
    valid = (side_lane < ALIGNED) | ((side_lane < ALIGNED + 64) == (p == 0))
    g_rows = jnp.where(valid, gp[...].astype(jnp.float32), 0.0).reshape(8, 8, HALF)
    u_rows = jnp.where(valid, up[...].astype(jnp.float32), 0.0).reshape(8, 8, HALF)
    none = jnp.zeros_like(g_rows)
    proj[...] = jnp.concatenate(
        [jnp.concatenate([g_rows, none], axis=2), jnp.concatenate([none, u_rows], axis=2)], axis=1
    ).reshape(2 * RANK, 2 * HALF).astype(jnp.bfloat16)

    z_wait(1, 0)
    w1_wait(1)
    w1_wait(3)
    w1_wait(2)
    sib_send(0, 0)
    local[2].wait()
    in_t[...] = contract_last(inp[...], tok[...]).astype(jnp.bfloat16)
    z_wait(2, 0)
    t1_wait(0)
    z_wait(1, 1)
    z_wait(1, 3)
    t2_wait(0)
    z_wait(3, 0)
    t1_wait(1)
    z_wait(1, 2)
    sib_send(1, 1)
    sib_send(2, -1)
    sib_wait(0, 0)
    own(0, True)
    z_wait(2, 1)
    t1_wait(2)
    off_pair = pl.multiple_of((1 - p) * HALF, 128)
    send(hg_hbm.at[:, pl.ds(off_pair, ALIGNED)], hgp.at[:, pl.ds(0, ALIGNED)], hg_s.at[0], hg_r.at[0], pair)
    send(hg_hbm.at[:, pl.ds(ALIGNED, 128)], hgp.at[:, pl.ds(ALIGNED, 128)], hg_s.at[1], hg_r.at[1], pair)
    x_wait(0, True)
    t2_wait(1)
    x_wait(0, False)
    z_wait(2, 3)
    x_wait(1, True)
    t2_wait(2)
    z_wait(2, 2)
    sib_send(3, 2)
    sib_send(4, -2)
    x_wait(1, False)
    x_wait(2, True)
    far_wait(0)
    sib_wait(1, 1)
    own(1)
    z_wait(3, 1)
    x_wait(2, False)
    sib_wait(2, -1)
    own(-1)
    z_wait(3, 3)
    far_wait(1)
    sib_wait(3, 2)
    own(2)
    z_wait(3, 2)
    sib_send(5, 3)
    sib_send(6, -3)
    sib_wait(4, -2)
    own(-2)
    far_wait(2)
    paired(0, True)
    paired(1)
    z_wait(4, 0)
    sib_send(7, 4, 0)
    z_wait(4, 1)
    sib_send(8, 4, 1)
    paired(-1)
    paired(2)
    paired(-2)
    z_wait(4, 3)
    sib_send(9, 4, 3)
    z_wait(4, 2)
    sib_send(10, 4, 2)
    sib_wait(5, 3)
    own(3)
    paired(3)
    sib_wait(6, -3)
    own(-3)
    paired(-3)
    for i, k in enumerate((0, 1, 3, 2)):
        sib_wait(7 + i, 4, k)
    own(4)
    paired(4)

    def gradients(held, row):
        @pl.loop(0, ROWS // 64)
        def _(j):
            r = pl.multiple_of(j * 64, 64)
            here = pl.ds(row + r, 64)
            mid = acc[here, ALIGNED:HALF]
            gate = jnp.concatenate([acc[here, :ALIGNED], mid], axis=1)
            up_ = jnp.concatenate([acc[here, HALF:], pltpu.roll(mid, 64, 1)], axis=1)
            cot = held[pl.ds(r, 64), :].astype(jnp.float32)
            sig = 0.5 * jnp.tanh(0.5 * gate) + 0.5
            scaled = cot * sig
            grads[here, :HALF] = (scaled * up_ * (1.0 + gate * (1.0 - sig))).astype(jnp.bfloat16)
            grads[here, HALF:] = (scaled * gate).astype(jnp.bfloat16)

    for n in range(2):
        landed(hgp.at[:, pl.ds(n * ALIGNED, (ALIGNED, 128)[n])], hg_s.at[n], hg_r.at[n])
    gradients(hgp, ROWS)
    parts[1] = contract_last(proj[...], grads[ROWS:, :]).astype(jnp.bfloat16)
    for k in range(8):
        j = (t + k) % 8
        rows = pl.ds(pl.multiple_of(j * 16, 16), 16)
        send(parts.at[1, rows], arrived.at[8 + k], rs_s.at[8 + k], rs_r.at[8 + k], (pair_dp, j))
    gradients(hgo, 0)
    parts[0] = contract_last(proj[...], grads[:ROWS, :]).astype(jnp.bfloat16)
    for k in range(1, 8):
        j = (t + k) % 8
        rows = pl.ds(pl.multiple_of(j * 16, 16), 16)
        send(parts.at[0, rows], arrived.at[k], rs_s.at[k], rs_r.at[k], (dp, j))
    side = parts[0, pl.ds(pl.multiple_of(t * 16, 16), 16), :].astype(jnp.float32)
    for k in (*range(8, 16), *range(1, 8)):
        landed(arrived.at[k], rs_s.at[k], rs_r.at[k])
        side += arrived[k].astype(jnp.float32)
    side = side.astype(jnp.bfloat16)

    slot = lax.broadcasted_iota(jnp.int32, (RANK, ROWS), 1)
    held = in_t[...]
    for n in range(2):
        used = (slot >= n * DOC_LEN) & (slot < n * DOC_LEN + len_ref[n])
        features = 0.0625 * contract_last(jnp.where(used, held, jnp.zeros_like(held)), side)
        og_ref[n] = features[:, :8]
        ou_ref[n] = features[:, 8:]

    for copy in started:
        copy.wait_send()


def shards(tokens, doc_lengths, gate_weight, up_weight, hidden_grad, in_projector, gate_projector, up_projector):
    bf, f32 = jnp.bfloat16, jnp.float32
    dma = pltpu.SemaphoreType.DMA
    anywhere = pl.BlockSpec(memory_space=pl.ANY)
    out = jax.ShapeDtypeStruct((2, RANK, 8), f32)
    pairs = [10, 3, 3, 16, 16, 16, 16, 11, 11, 3, 3, 3, 3, 9, 9, 9, 9, 2, 2, 16, 16]
    return pl.pallas_call(
        kernel,
        out_shape=(out, out),
        in_specs=[pl.BlockSpec(memory_space=pltpu.SMEM)] + [anywhere] * 7,
        out_specs=(pl.BlockSpec(memory_space=pltpu.VMEM),) * 2,
        scratch_shapes=[
            pltpu.VMEM((ROWS, D), bf),
            pltpu.VMEM((ROWS, D), bf),
            pltpu.VMEM((SHARD, COLS), bf),
            pltpu.VMEM((SHARD, COLS), bf),
            pltpu.VMEM((SHARD, COLS), bf),
            pltpu.VMEM((ZS, YS, 2, SHARD, COLS), bf),
            pltpu.VMEM((ROWS, HALF), bf),
            pltpu.VMEM((ROWS, HALF), bf),
            pltpu.VMEM((RANK, D), bf),
            pltpu.VMEM((RANK, HALF), bf),
            pltpu.VMEM((RANK, HALF), bf),
            pltpu.VMEM((2 * ROWS, COLS), f32),
            pltpu.VMEM((2 * ROWS, 2 * HALF), bf),
            pltpu.VMEM((2 * RANK, 2 * HALF), bf),
            pltpu.VMEM((2, 2 * RANK, ROWS), bf),
            pltpu.VMEM((16, 16, ROWS), bf),
            pltpu.VMEM((RANK, ROWS), bf),
        ]
        + [dma((n,)) for n in pairs],
        compiler_params=pltpu.CompilerParams(
            collective_id=0, has_side_effects=True, vmem_limit_bytes=48 * 2**20
        ),
        name="features",
    )(
        doc_lengths, tokens, gate_weight, up_weight, hidden_grad,
        in_projector, gate_projector, up_projector,
    )


def solution(mesh):
    placed = (
        P("dp", None),
        P("dp"),
        P("dp", "tensor"),
        P("dp", "tensor"),
        P("dp", "tensor"),
        P(),
        P(None, "tensor"),
        P(None, "tensor"),
    )
    return jax.shard_map(
        shards,
        mesh=mesh,
        in_specs=placed,
        out_specs=(P("dp", None, "tensor"), P("dp", None, "tensor")),
        check_vma=False,
    )
```

```python
import jax
import jax.numpy as jnp
from jax import lax
from jax.experimental import pallas as pl
from jax.experimental.pallas import tpu as pltpu
from jax.sharding import PartitionSpec as P

MESH = pl.DeviceIdType.MESH
DOC_LEN = 192
ROWS = 384
D = 4096
COLS = 896
RANK = 64
ALIGNED = 384
HALF = 512
ZS, YS = 8, 4
BLOCK = D // ZS
SHARD = 64
PIECE = 16
SUBS = 3
ORDER = (0, 1, 3, 2)
LAST_RIGHT, LAST_LEFT = (0, 3), (1, 2)
SIB = tuple((dz, None) for dz in (0, 1, -1, 2, -2, 3, -3)) + tuple((4, k) for k in ORDER)
PLAN = (
    ("in",), ("z", 1, 0), ("w1", 1), ("w1", 3), ("w1", 2), ("z", 2, 0), ("t1", 0), ("sib", 0), ("own", 0),
    ("z", 1, 1), ("z", 1, 3), ("t2", 0), ("xn", 0), ("z", 1, 2), ("t1", 1), ("sib", 1), ("z", 3, 0),
    ("own", 1), ("sib", 2), ("own", -1), ("xf", 0), ("z", 2, 1), ("z", 2, 3), ("fr", 0), ("t2", 1),
    ("z", 2, 2), ("fl", 0), ("t1", 2), ("xn", 1), ("sib", 3), ("z", 4, 0), ("own", 2), ("xf", 1), ("sib", 4),
    ("own", -2), ("sib", 7), ("z", 3, 1), ("t2", 2), ("xn", 2), ("z", 3, 3), ("fl", 1), ("fr", 1),
    ("z", 3, 2), ("z", 4, 1), ("xf", 2), ("sib", 5), ("own", 3), ("z", 4, 3), ("sib", 6), ("own", -3),
    ("sib", 8), ("sib", 9), ("fr", 2), ("z", 4, 2), ("sib", 10), ("own", 4), ("fl", 2), ("paired", 0),
    ("paired", 1), ("paired", -1), ("paired", 2), ("paired", -2), ("paired", 3), ("paired", -3),
    ("paired", 4),
)
LIMIT = {"zr": 9, "zl": 9, "xr": 9, "xl": 9, "y": 1, "t2": 9}


def contract_last(left, right):
    return lax.dot_general(
        left, right, (((1,), (1,)), ((), ())), preferred_element_type=jnp.float32
    )


def kernel(
    len_hbm, tok_hbm, gw_hbm, uw_hbm, hg_hbm, inp_hbm, gp_hbm, up_hbm,
    og_ref, ou_ref,
    tok, tokp, gw, uw, other, w5, hgo, hgp, inp, gp, up,
    acc, grads, proj, parts, arrived, in_t, len_ref,
    loc_sem, w1_s, w1_r, zr_s, zr_r, zl_s, zl_r, sib_s, sib_r,
    t1_s, t1_r, t2_s, t2_r, xr_s, xr_r, xl_s, xl_r, hg_s, hg_r, rs_s, rs_r,
):
    dp, t = lax.axis_index("dp"), lax.axis_index("tensor")
    z, yh, c = dp // 8, (dp // 2) % YS, dp % 2
    yl, x = t // 4, t % 4
    p = yh % 2
    yhp = yh + 1 - 2 * p

    def at(z_, yh_, c_, yl_, x_):
        return (z_ * 8 + yh_ * 2 + c_, yl_ * 4 + x_)

    z_right, z_left = at((z + 1) % ZS, yh, c, yl, x), at((z + ZS - 1) % ZS, yh, c, yl, x)
    sibling = at(z, yh, 1 - c, yl, x)
    pair = at(z, yhp, c, yl, x)
    y_sib = at(z, yh, c, 1 - yl, x)
    x_right, x_left = at(z, yh, c, yl, (x + 1) % 4), at(z, yh, c, yl, (x + 3) % 4)
    pair_dp = pair[0]

    off = pl.multiple_of(p * HALF, 128)
    local = [
        pltpu.make_async_copy(gw_hbm, gw, loc_sem.at[0]),
        pltpu.make_async_copy(uw_hbm, uw, loc_sem.at[1]),
        pltpu.make_async_copy(tok_hbm, tok, loc_sem.at[2]),
        pltpu.make_async_copy(hg_hbm.at[:, pl.ds(off, ALIGNED)], hgo.at[:, pl.ds(0, ALIGNED)], loc_sem.at[3]),
        pltpu.make_async_copy(hg_hbm.at[:, pl.ds(ALIGNED, 128)], hgo.at[:, pl.ds(ALIGNED, 128)], loc_sem.at[4]),
        pltpu.make_async_copy(inp_hbm, inp, loc_sem.at[5]),
        pltpu.make_async_copy(gp_hbm.at[:, pl.ds(off, ALIGNED)], gp.at[:, pl.ds(0, ALIGNED)], loc_sem.at[6]),
        pltpu.make_async_copy(gp_hbm.at[:, pl.ds(ALIGNED, 128)], gp.at[:, pl.ds(ALIGNED, 128)], loc_sem.at[7]),
        pltpu.make_async_copy(up_hbm.at[:, pl.ds(off, ALIGNED)], up.at[:, pl.ds(0, ALIGNED)], loc_sem.at[8]),
        pltpu.make_async_copy(up_hbm.at[:, pl.ds(ALIGNED, 128)], up.at[:, pl.ds(ALIGNED, 128)], loc_sem.at[9]),
        pltpu.make_async_copy(len_hbm, len_ref, loc_sem.at[10]),
    ]
    for copy in local:
        copy.start()

    barrier = pltpu.get_barrier_semaphore()
    greeted = [z_right, z_left, sibling, at(z, (yh + 2) % YS, c, yl, x), at(z, (yhp + 2) % YS, c, yl, x)]
    for who in greeted:
        pl.semaphore_signal(barrier, inc=1, device_id=who, device_id_type=MESH)
    for k in range(1, 8):
        pl.semaphore_signal(barrier, inc=1, device_id=(dp, (t + k) % 8), device_id_type=MESH)
    for k in range(8):
        pl.semaphore_signal(barrier, inc=1, device_id=(pair_dp, (t + k) % 8), device_id_type=MESH)

    local[0].wait()
    local[1].wait()
    lane = lax.broadcasted_iota(jnp.int32, (SHARD, 128), 1)
    g3 = gw[:, ALIGNED:HALF].astype(jnp.float32)
    u3 = pltpu.roll(uw[:, ALIGNED:HALF].astype(jnp.float32), 64, 1)
    mid0 = jnp.where(lane < 64, g3, u3).astype(jnp.bfloat16)
    mid1 = jnp.where(lane < 64, u3, g3).astype(jnp.bfloat16)

    def pack(even):
        lo = jnp.concatenate([gw[:, :ALIGNED], mid0, uw[:, :ALIGNED]], axis=1)
        hi = jnp.concatenate([gw[:, HALF:], mid1, uw[:, HALF:]], axis=1)
        return jnp.where(even, lo, hi)

    w5[z, yh, c] = pack(p == 0)
    other[...] = pack(p == 1)

    pl.semaphore_wait(barrier, len(greeted) + 15)

    started = []

    def send(src, dst, ss, rs, who):
        copy = pltpu.make_async_remote_copy(
            src_ref=src, dst_ref=dst, send_sem=ss, recv_sem=rs, device_id=who, device_id_type=MESH
        )
        copy.start()
        started.append(copy)

    flying, queued = dict.fromkeys(LIMIT, 0), {stream: [] for stream in LIMIT}

    def pump(stream):
        while queued[stream] and flying[stream] < LIMIT[stream]:
            flying[stream] += 1
            send(*queued[stream].pop(0))

    def post(stream, *copy):
        queued[stream].append(copy)
        pump(stream)

    def done(*streams):
        for stream in streams:
            flying[stream] -= 1
            pump(stream)

    def landed(dst, ss, rs):
        pltpu.make_async_remote_copy(
            src_ref=dst, dst_ref=dst, send_sem=ss, recv_sem=rs, device_id=sibling, device_id_type=MESH
        ).wait_recv()

    def chunk(dz, k):
        return w5.at[(z + dz + 2 * ZS) % ZS, (yh + k) % YS, c]

    def z_send_right(s, k):
        i = (s - 1) * 4 + k
        ref = chunk(1 - s, k)
        post("zr", ref, ref, zr_s.at[i], zr_r.at[i], z_right)

    def z_send_left(s, k):
        i = (s - 1) * 4 + k
        ref = chunk(s - 1, k)
        post("zl", ref, ref, zl_s.at[i], zl_r.at[i], z_left)

    def pass_on(s, k):
        if s < 4 or k in LAST_RIGHT:
            z_send_right(s, k)
        if s < 4 or k in LAST_LEFT:
            z_send_left(s, k)

    def z_wait(s, k):
        i = (s - 1) * 4 + k
        if s < 4 or k in LAST_RIGHT:
            landed(chunk(-s, k), zr_s.at[i], zr_r.at[i])
            done("zr")
        if s < 4 or k in LAST_LEFT:
            landed(chunk(s, k), zl_s.at[i], zl_r.at[i])
            done("zl")
        if s < 4:
            pass_on(s + 1, k)

    def sib_send(i, dz, k=None):
        ref = w5.at[(z + dz + ZS) % ZS, :, c] if k is None else chunk(dz, k)
        send(ref, ref, sib_s.at[i], sib_r.at[i], sibling)

    def sib_wait(i, dz, k=None):
        zz = (z + dz + ZS) % ZS
        ref = w5.at[zz, :, 1 - c] if k is None else w5.at[zz, (yh + k) % YS, 1 - c]
        landed(ref, sib_s.at[i], sib_r.at[i])

    def piece(xx, yy, i):
        start = 96 * ((x + xx + 4) % 4) + 48 * yy + PIECE * i
        return pl.ds(pl.multiple_of(start, PIECE), PIECE)

    def t1_send(i):
        rows = piece(0, yl, i)
        post("y", tok_hbm.at[rows], tokp.at[rows], t1_s.at[i], t1_r.at[i], pair)

    def x_sends(ref, n):
        post("xr", ref, ref, xr_s.at[n], xr_r.at[n], x_right)
        post("xl", ref, ref, xl_s.at[n], xl_r.at[n], x_left)

    def t1_wait(i):
        ref = tokp.at[piece(0, yl, i)]
        landed(ref, t1_s.at[i], t1_r.at[i])
        done("y")
        post("t2", ref, ref, t2_s.at[i], t2_r.at[i], y_sib)
        x_sends(ref, i)
        if i == SUBS - 1:
            send_cotangent()

    def t2_wait(i):
        ref = tokp.at[piece(0, 1 - yl, i)]
        landed(ref, t2_s.at[i], t2_r.at[i])
        done("t2")
        x_sends(ref, SUBS + i)

    def x_near(i):
        ref_l, ref_r = tokp.at[piece(-1, yl, i)], tokp.at[piece(1, yl, i)]
        landed(ref_l, xr_s.at[i], xr_r.at[i])
        landed(ref_r, xl_s.at[i], xl_r.at[i])
        done("xr", "xl")
        m = 2 * SUBS + i
        post("xr", ref_l, ref_l, xr_s.at[m], xr_r.at[m], x_right)

    def x_other(i):
        n = SUBS + i
        ref_l, ref_r = tokp.at[piece(-1, 1 - yl, i)], tokp.at[piece(1, 1 - yl, i)]
        landed(ref_l, xr_s.at[n], xr_r.at[n])
        landed(ref_r, xl_s.at[n], xl_r.at[n])
        done("xr", "xl")
        m = 2 * SUBS + i
        post("xl", ref_r, ref_r, xl_s.at[m], xl_r.at[m], x_left)

    def x_far_right(i):
        m = 2 * SUBS + i
        landed(tokp.at[piece(-2, yl, i)], xr_s.at[m], xr_r.at[m])
        done("xr")

    def x_far_left(i):
        m = 2 * SUBS + i
        landed(tokp.at[piece(2, 1 - yl, i)], xl_s.at[m], xl_r.at[m])
        done("xl")

    def product(held, row, zz, first=False):
        columns = pl.ds(pl.multiple_of(zz * BLOCK, BLOCK), BLOCK)
        term = jnp.dot(
            held[:, columns], w5[zz].reshape(BLOCK, COLS), preferred_element_type=jnp.float32
        )
        if first:
            acc[row : row + ROWS, :] = term
        else:
            acc[row : row + ROWS, :] += term

    def own(dz, first=False):
        product(tok, 0, (z + dz + ZS) % ZS, first)

    def paired(dz, first=False):
        product(tokp, ROWS, (z + dz + ZS) % ZS, first)

    pass_on(1, 0)
    mine = w5.at[z, yh, c]
    for d in (1, 3):
        send(other, mine, w1_s.at[d - 1], w1_r.at[3 - d], at(z, (yh + d) % YS, c, yl, x))
    send(mine, mine, w1_s.at[1], w1_r.at[1], at(z, (yh + 2) % YS, c, yl, x))
    for i in range(SUBS):
        t1_send(i)

    def send_cotangent():
        off_pair = pl.multiple_of((1 - p) * HALF, 128)
        send(hg_hbm.at[:, pl.ds(off_pair, ALIGNED)], hgp.at[:, pl.ds(0, ALIGNED)], hg_s.at[0], hg_r.at[0], pair)
        send(hg_hbm.at[:, pl.ds(ALIGNED, 128)], hgp.at[:, pl.ds(ALIGNED, 128)], hg_s.at[1], hg_r.at[1], pair)

    def w1_wait(k):
        landed(chunk(0, k), w1_s.at[k - 1], w1_r.at[k - 1])
        pass_on(1, k)

    for copy in local[3:]:
        copy.wait()
    side_lane = lax.broadcasted_iota(jnp.int32, (RANK, HALF), 1)
    valid = (side_lane < ALIGNED) | ((side_lane < ALIGNED + 64) == (p == 0))
    g_rows = jnp.where(valid, gp[...].astype(jnp.float32), 0.0).reshape(8, 8, HALF)
    u_rows = jnp.where(valid, up[...].astype(jnp.float32), 0.0).reshape(8, 8, HALF)
    none = jnp.zeros_like(g_rows)
    proj[...] = jnp.concatenate(
        [jnp.concatenate([g_rows, none], axis=2), jnp.concatenate([none, u_rows], axis=2)], axis=1
    ).reshape(2 * RANK, 2 * HALF).astype(jnp.bfloat16)

    seen = set()

    def ring(s, k):
        z_wait(s, k)
        if s == 4:
            sib_send(7 + ORDER.index(k), 4, k)
        elif all(("z", s, other_k) in seen for other_k in range(4)):
            sib_send(2 * s - 1, s)
            sib_send(2 * s, -s)

    def first_hop(k):
        w1_wait(k)
        if all(("w1", other_k) in seen for other_k in (1, 2, 3)):
            sib_send(0, 0)

    def project_inputs():
        local[2].wait()
        in_t[...] = contract_last(inp[...], tok[...]).astype(jnp.bfloat16)

    actions = {
        "z": ring,
        "w1": first_hop,
        "t1": t1_wait,
        "t2": t2_wait,
        "xn": x_near,
        "xf": x_other,
        "fr": x_far_right,
        "fl": x_far_left,
        "sib": lambda i: sib_wait(i, SIB[i][0], SIB[i][1]),
        "in": project_inputs,
        "own": lambda dz: own(dz, dz == 0),
        "paired": lambda dz: paired(dz, dz == 0),
    }
    for name, *which in PLAN:
        seen.add((name, *which))
        actions[name](*which)

    def gradients(held, row):
        @pl.loop(0, ROWS // 64)
        def _(j):
            r = pl.multiple_of(j * 64, 64)
            here = pl.ds(row + r, 64)
            mid = acc[here, ALIGNED:HALF]
            gate = jnp.concatenate([acc[here, :ALIGNED], mid], axis=1)
            up_ = jnp.concatenate([acc[here, HALF:], pltpu.roll(mid, 64, 1)], axis=1)
            cot = held[pl.ds(r, 64), :].astype(jnp.float32)
            sig = 0.5 * jnp.tanh(0.5 * gate) + 0.5
            scaled = cot * sig
            grads[here, :HALF] = (scaled * up_ * (1.0 + gate * (1.0 - sig))).astype(jnp.bfloat16)
            grads[here, HALF:] = (scaled * gate).astype(jnp.bfloat16)

    for n in range(2):
        landed(hgp.at[:, pl.ds(n * ALIGNED, (ALIGNED, 128)[n])], hg_s.at[n], hg_r.at[n])
    gradients(hgp, ROWS)
    parts[1] = contract_last(proj[...], grads[ROWS:, :]).astype(jnp.bfloat16)
    for k in range(8):
        j = (t + k) % 8
        rows = pl.ds(pl.multiple_of(j * 16, 16), 16)
        send(parts.at[1, rows], arrived.at[8 + k], rs_s.at[8 + k], rs_r.at[8 + k], (pair_dp, j))
    gradients(hgo, 0)
    parts[0] = contract_last(proj[...], grads[:ROWS, :]).astype(jnp.bfloat16)
    for k in range(1, 8):
        j = (t + k) % 8
        rows = pl.ds(pl.multiple_of(j * 16, 16), 16)
        send(parts.at[0, rows], arrived.at[k], rs_s.at[k], rs_r.at[k], (dp, j))
    side = parts[0, pl.ds(pl.multiple_of(t * 16, 16), 16), :].astype(jnp.float32)
    for k in (*range(8, 16), *range(1, 8)):
        landed(arrived.at[k], rs_s.at[k], rs_r.at[k])
        side += arrived[k].astype(jnp.float32)
    side = side.astype(jnp.bfloat16)

    slot = lax.broadcasted_iota(jnp.int32, (RANK, ROWS), 1)
    held = in_t[...]
    for n in range(2):
        used = (slot >= n * DOC_LEN) & (slot < n * DOC_LEN + len_ref[n])
        features = 0.0625 * contract_last(side, jnp.where(used, held, jnp.zeros_like(held)))
        og_ref[n] = features[:8]
        ou_ref[n] = features[8:]

    for copy in started:
        copy.wait_send()


def shards(tokens, doc_lengths, gate_weight, up_weight, hidden_grad, in_projector, gate_projector, up_projector):
    bf, f32 = jnp.bfloat16, jnp.float32
    dma = pltpu.SemaphoreType.DMA
    out = jax.ShapeDtypeStruct((2, 8, RANK), f32)
    pairs = [11, 3, 3, 16, 16, 16, 16, 11, 11, 3, 3, 3, 3, 9, 9, 9, 9, 2, 2, 16, 16]
    gate_features, up_features = pl.pallas_call(
        kernel,
        out_shape=(out, out),
        in_specs=[pl.BlockSpec(memory_space=pltpu.HBM)] * 8,
        out_specs=(pl.BlockSpec(memory_space=pltpu.VMEM),) * 2,
        scratch_shapes=[
            pltpu.VMEM((ROWS, D), bf),
            pltpu.VMEM((ROWS, D), bf),
            pltpu.VMEM((SHARD, COLS), bf),
            pltpu.VMEM((SHARD, COLS), bf),
            pltpu.VMEM((SHARD, COLS), bf),
            pltpu.VMEM((ZS, YS, 2, SHARD, COLS), bf),
            pltpu.VMEM((ROWS, HALF), bf),
            pltpu.VMEM((ROWS, HALF), bf),
            pltpu.VMEM((RANK, D), bf),
            pltpu.VMEM((RANK, HALF), bf),
            pltpu.VMEM((RANK, HALF), bf),
            pltpu.VMEM((2 * ROWS, COLS), f32),
            pltpu.VMEM((2 * ROWS, 2 * HALF), bf),
            pltpu.VMEM((2 * RANK, 2 * HALF), bf),
            pltpu.VMEM((2, 2 * RANK, ROWS), bf),
            pltpu.VMEM((16, 16, ROWS), bf),
            pltpu.VMEM((RANK, ROWS), bf),
            pltpu.SMEM((2,), jnp.int32),
        ]
        + [dma((n,)) for n in pairs],
        compiler_params=pltpu.CompilerParams(
            collective_id=0, has_side_effects=True, vmem_limit_bytes=58 * 2**20
        ),
        name="features",
    )(
        doc_lengths, tokens, gate_weight, up_weight, hidden_grad,
        in_projector, gate_projector, up_projector,
    )
    return gate_features.transpose(0, 2, 1), up_features.transpose(0, 2, 1)


def solution(mesh):
    placed = (
        P("dp", None),
        P("dp"),
        P("dp", "tensor"),
        P("dp", "tensor"),
        P("dp", "tensor"),
        P(),
        P(None, "tensor"),
        P(None, "tensor"),
    )
    return jax.shard_map(
        shards,
        mesh=mesh,
        in_specs=placed,
        out_specs=(P("dp", None, "tensor"), P("dp", None, "tensor")),
        check_vma=False,
    )
```

```python
import jax
import jax.numpy as jnp
from jax import lax
from jax.experimental import pallas as pl
from jax.experimental.pallas import tpu as pltpu
from jax.sharding import PartitionSpec as P

MESH = pl.DeviceIdType.MESH
DOC_LEN = 192
ROWS = 384
D = 4096
COLS = 896
RANK = 64
ALIGNED = 384
HALF = 512
ZS, YS = 8, 4
BLOCK = D // ZS
SHARD = 64
PIECE = 16
SUBS = 3
ORDER = (0, 1, 3, 2)
LAST_RIGHT, LAST_LEFT = (0, 3), (1, 2)
SIB = tuple((dz, None) for dz in (0, 1, -1, 2, -2, 3, -3)) + tuple((4, k) for k in ORDER)
PLAN = (
    ("in",), ("z", 1, 0), ("w1", 1), ("w1", 3), ("w1", 2), ("t1", 0), ("z", 2, 0), ("sib", 0), ("z", 1, 1),
    ("z", 1, 3), ("t2", 0), ("xn", 0), ("t1", 1), ("z", 1, 2), ("sib", 1), ("z", 3, 0), ("xf", 0), ("sib", 2),
    ("mul", "own", -1, 1), ("z", 2, 1), ("t2", 1), ("fr", 0), ("z", 2, 3), ("t1", 2), ("fl", 0), ("xn", 1),
    ("z", 2, 2), ("sib", 3), ("z", 4, 0), ("xf", 1), ("mul", "own", 2, 2), ("t2", 2), ("sib", 4),
    ("mul", "own", -2, -2), ("sib", 7), ("z", 3, 1), ("xn", 2), ("z", 3, 3), ("fr", 1), ("fl", 1),
    ("z", 3, 2), ("z", 4, 1), ("xf", 2), ("sib", 5), ("mul", "own", 3, 3), ("z", 4, 3), ("sib", 6), ("fr", 2),
    ("mul", "own", -3, -3), ("sib", 8), ("sib", 9), ("z", 4, 2), ("sib", 10), ("fl", 2),
    ("mul", "pair", -3, 3), ("mul", "both", 4, 4), ("finish", 1), ("finish", 0),
)
LIMIT = {"zr": 9, "zl": 9, "xr": 9, "xl": 9, "y": 1, "t2": 9}


def contract_last(left, right):
    return lax.dot_general(
        left, right, (((1,), (1,)), ((), ())), preferred_element_type=jnp.float32
    )


def kernel(
    len_hbm, tok_hbm, gw_hbm, uw_hbm, hg_hbm, inp_hbm, gp_hbm, up_hbm,
    og_ref, ou_ref,
    toks, gw, uw, other, w5, hgo, hgp, inp, gp, up,
    acc, grads, proj, parts, arrived, in_t, len_ref,
    loc_sem, w1_s, w1_r, zr_s, zr_r, zl_s, zl_r, sib_s, sib_r,
    t1_s, t1_r, t2_s, t2_r, xr_s, xr_r, xl_s, xl_r, hg_s, hg_r, rs_s, rs_r,
):
    dp, t = lax.axis_index("dp"), lax.axis_index("tensor")
    z, yh, c = dp // 8, (dp // 2) % YS, dp % 2
    yl, x = t // 4, t % 4
    p = yh % 2
    yhp = yh + 1 - 2 * p

    def at(z_, yh_, c_, yl_, x_):
        return (z_ * 8 + yh_ * 2 + c_, yl_ * 4 + x_)

    z_right, z_left = at((z + 1) % ZS, yh, c, yl, x), at((z + ZS - 1) % ZS, yh, c, yl, x)
    sibling = at(z, yh, 1 - c, yl, x)
    pair = at(z, yhp, c, yl, x)
    y_sib = at(z, yh, c, 1 - yl, x)
    x_right, x_left = at(z, yh, c, yl, (x + 1) % 4), at(z, yh, c, yl, (x + 3) % 4)
    pair_dp = pair[0]

    off = pl.multiple_of(p * HALF, 128)
    local = [
        pltpu.make_async_copy(gw_hbm, gw, loc_sem.at[0]),
        pltpu.make_async_copy(uw_hbm, uw, loc_sem.at[1]),
        pltpu.make_async_copy(hg_hbm.at[:, pl.ds(off, ALIGNED)], hgo.at[:, pl.ds(0, ALIGNED)], loc_sem.at[3]),
        pltpu.make_async_copy(hg_hbm.at[:, pl.ds(ALIGNED, 128)], hgo.at[:, pl.ds(ALIGNED, 128)], loc_sem.at[4]),
        pltpu.make_async_copy(gp_hbm.at[:, pl.ds(off, ALIGNED)], gp.at[:, pl.ds(0, ALIGNED)], loc_sem.at[6]),
        pltpu.make_async_copy(gp_hbm.at[:, pl.ds(ALIGNED, 128)], gp.at[:, pl.ds(ALIGNED, 128)], loc_sem.at[7]),
        pltpu.make_async_copy(up_hbm.at[:, pl.ds(off, ALIGNED)], up.at[:, pl.ds(0, ALIGNED)], loc_sem.at[8]),
        pltpu.make_async_copy(up_hbm.at[:, pl.ds(ALIGNED, 128)], up.at[:, pl.ds(ALIGNED, 128)], loc_sem.at[9]),
        pltpu.make_async_copy(len_hbm, len_ref, loc_sem.at[2]),
    ]
    def width(r):
        return pl.ds(pl.multiple_of((z + r + 5) % ZS * BLOCK, BLOCK), BLOCK)

    for r in range(ZS):
        here = pl.ds(r * BLOCK, BLOCK)
        local.append(
            pltpu.make_async_copy(tok_hbm.at[:, width(r)], toks.at[pl.ds(0, ROWS), here], loc_sem.at[10 + r])
        )
    for r in range(ZS):
        here = pl.ds(r * BLOCK, BLOCK)
        local.append(pltpu.make_async_copy(inp_hbm.at[:, width(r)], inp.at[:, here], loc_sem.at[18 + r]))
    for copy in local:
        copy.start()

    barrier = pltpu.get_barrier_semaphore()
    greeted = [z_right, z_left, sibling, at(z, (yh + 2) % YS, c, yl, x), at(z, (yhp + 2) % YS, c, yl, x)]
    for who in greeted:
        pl.semaphore_signal(barrier, inc=1, device_id=who, device_id_type=MESH)
    for k in range(1, 8):
        pl.semaphore_signal(barrier, inc=1, device_id=(dp, (t + k) % 8), device_id_type=MESH)
    for k in range(8):
        pl.semaphore_signal(barrier, inc=1, device_id=(pair_dp, (t + k) % 8), device_id_type=MESH)

    local[0].wait()
    local[1].wait()
    lane = lax.broadcasted_iota(jnp.int32, (SHARD, 128), 1)
    g3 = gw[:, ALIGNED:HALF].astype(jnp.float32)
    u3 = pltpu.roll(uw[:, ALIGNED:HALF].astype(jnp.float32), 64, 1)
    mid0 = jnp.where(lane < 64, g3, u3).astype(jnp.bfloat16)
    mid1 = jnp.where(lane < 64, u3, g3).astype(jnp.bfloat16)

    def pack(even):
        lo = jnp.concatenate([gw[:, :ALIGNED], mid0, uw[:, :ALIGNED]], axis=1)
        hi = jnp.concatenate([gw[:, HALF:], mid1, uw[:, HALF:]], axis=1)
        return jnp.where(even, lo, hi)

    w5[3, yh, c] = pack(p == 0)
    other[...] = pack(p == 1)

    pl.semaphore_wait(barrier, len(greeted) + 15)

    started = []

    def send(src, dst, ss, rs, who):
        copy = pltpu.make_async_remote_copy(
            src_ref=src, dst_ref=dst, send_sem=ss, recv_sem=rs, device_id=who, device_id_type=MESH
        )
        copy.start()
        started.append(copy)

    flying, queued = dict.fromkeys(LIMIT, 0), {stream: [] for stream in LIMIT}

    def pump(stream):
        while queued[stream] and flying[stream] < LIMIT[stream]:
            flying[stream] += 1
            send(*queued[stream].pop(0))

    def post(stream, *copy):
        queued[stream].append(copy)
        pump(stream)

    def done(*streams):
        for stream in streams:
            flying[stream] -= 1
            pump(stream)

    def landed(dst, ss, rs):
        pltpu.make_async_remote_copy(
            src_ref=dst, dst_ref=dst, send_sem=ss, recv_sem=rs, device_id=sibling, device_id_type=MESH
        ).wait_recv()

    def chunk(dz, k):
        return w5.at[3 + dz, (yh + k) % YS, c]

    def z_send_right(s, k):
        i = (s - 1) * 4 + k
        post("zr", chunk(1 - s, k), chunk(-s if s < 4 else 4, k), zr_s.at[i], zr_r.at[i], z_right)

    def z_send_left(s, k):
        i = (s - 1) * 4 + k
        post("zl", chunk(s - 1, k), chunk(s, k), zl_s.at[i], zl_r.at[i], z_left)

    def pass_on(s, k):
        if s < 4 or k in LAST_RIGHT:
            z_send_right(s, k)
        if s < 4 or k in LAST_LEFT:
            z_send_left(s, k)

    def z_wait(s, k):
        i = (s - 1) * 4 + k
        if s < 4 or k in LAST_RIGHT:
            landed(chunk(-s if s < 4 else 4, k), zr_s.at[i], zr_r.at[i])
            done("zr")
        if s < 4 or k in LAST_LEFT:
            landed(chunk(s, k), zl_s.at[i], zl_r.at[i])
            done("zl")
        if s < 4:
            pass_on(s + 1, k)

    def sib_send(i, dz, k=None):
        ref = w5.at[3 + dz, :, c] if k is None else chunk(dz, k)
        send(ref, ref, sib_s.at[i], sib_r.at[i], sibling)

    def sib_wait(i, dz, k=None):
        ref = w5.at[3 + dz, :, 1 - c] if k is None else w5.at[3 + dz, (yh + k) % YS, 1 - c]
        landed(ref, sib_s.at[i], sib_r.at[i])

    def piece(xx, yy, i, base=ROWS):
        start = base + 96 * ((x + xx + 4) % 4) + 48 * yy + PIECE * i
        return pl.ds(pl.multiple_of(start, PIECE), PIECE)

    def t1_send(i):
        post("y", toks.at[piece(0, yl, i, 0)], toks.at[piece(0, yl, i)], t1_s.at[i], t1_r.at[i], pair)

    def x_sends(ref, n):
        post("xr", ref, ref, xr_s.at[n], xr_r.at[n], x_right)
        post("xl", ref, ref, xl_s.at[n], xl_r.at[n], x_left)

    def t1_wait(i):
        ref = toks.at[piece(0, yl, i)]
        landed(ref, t1_s.at[i], t1_r.at[i])
        done("y")
        post("t2", ref, ref, t2_s.at[i], t2_r.at[i], y_sib)
        x_sends(ref, i)
        if i == SUBS - 1:
            send_cotangent()

    def t2_wait(i):
        ref = toks.at[piece(0, 1 - yl, i)]
        landed(ref, t2_s.at[i], t2_r.at[i])
        done("t2")
        x_sends(ref, SUBS + i)

    def x_near(i):
        ref_l, ref_r = toks.at[piece(-1, yl, i)], toks.at[piece(1, yl, i)]
        landed(ref_l, xr_s.at[i], xr_r.at[i])
        landed(ref_r, xl_s.at[i], xl_r.at[i])
        done("xr", "xl")
        m = 2 * SUBS + i
        post("xr", ref_l, ref_l, xr_s.at[m], xr_r.at[m], x_right)

    def x_other(i):
        n = SUBS + i
        ref_l, ref_r = toks.at[piece(-1, 1 - yl, i)], toks.at[piece(1, 1 - yl, i)]
        landed(ref_l, xr_s.at[n], xr_r.at[n])
        landed(ref_r, xl_s.at[n], xl_r.at[n])
        done("xr", "xl")
        m = 2 * SUBS + i
        post("xl", ref_r, ref_r, xl_s.at[m], xl_r.at[m], x_left)

    def x_far_right(i):
        m = 2 * SUBS + i
        landed(toks.at[piece(-2, yl, i)], xr_s.at[m], xr_r.at[m])
        done("xr")

    def x_far_left(i):
        m = 2 * SUBS + i
        landed(toks.at[piece(2, 1 - yl, i)], xl_s.at[m], xl_r.at[m])
        done("xl")

    fresh = [True, True]

    def product(who, a, b):
        lo, hi = {"own": (0, ROWS), "pair": (ROWS, 2 * ROWS), "both": (0, 2 * ROWS)}[who]
        depth = (b - a + 1) * BLOCK
        term = jnp.dot(
            toks[lo:hi, (a + 3) * BLOCK : (b + 4) * BLOCK],
            w5[a + 3 : b + 4].reshape(depth, COLS),
            preferred_element_type=jnp.float32,
        )
        if fresh[lo // ROWS]:
            acc[lo:hi, :] = term
        else:
            acc[lo:hi, :] += term
        for n in range(lo // ROWS, hi // ROWS):
            fresh[n] = False

    pass_on(1, 0)
    for copy in local[2:]:
        copy.wait()
    mine = w5.at[3, yh, c]
    for d in (1, 3):
        send(other, mine, w1_s.at[d - 1], w1_r.at[3 - d], at(z, (yh + d) % YS, c, yl, x))
    send(mine, mine, w1_s.at[1], w1_r.at[1], at(z, (yh + 2) % YS, c, yl, x))
    for i in range(SUBS):
        t1_send(i)

    def send_cotangent():
        off_pair = pl.multiple_of((1 - p) * HALF, 128)
        send(hg_hbm.at[:, pl.ds(off_pair, ALIGNED)], hgp.at[:, pl.ds(0, ALIGNED)], hg_s.at[0], hg_r.at[0], pair)
        send(hg_hbm.at[:, pl.ds(ALIGNED, 128)], hgp.at[:, pl.ds(ALIGNED, 128)], hg_s.at[1], hg_r.at[1], pair)

    def w1_wait(k):
        landed(chunk(0, k), w1_s.at[k - 1], w1_r.at[k - 1])
        pass_on(1, k)

    side_lane = lax.broadcasted_iota(jnp.int32, (RANK, HALF), 1)
    valid = (side_lane < ALIGNED) | ((side_lane < ALIGNED + 64) == (p == 0))
    g_rows = jnp.where(valid, gp[...].astype(jnp.float32), 0.0).reshape(8, 8, HALF)
    u_rows = jnp.where(valid, up[...].astype(jnp.float32), 0.0).reshape(8, 8, HALF)
    none = jnp.zeros_like(g_rows)
    proj[...] = jnp.concatenate(
        [jnp.concatenate([g_rows, none], axis=2), jnp.concatenate([none, u_rows], axis=2)], axis=1
    ).reshape(2 * RANK, 2 * HALF).astype(jnp.bfloat16)

    def gradients(held, row):
        @pl.loop(0, ROWS // 64)
        def _(j):
            r = pl.multiple_of(j * 64, 64)
            here = pl.ds(row + r, 64)
            mid = acc[here, ALIGNED:HALF]
            gate = jnp.concatenate([acc[here, :ALIGNED], mid], axis=1)
            up_ = jnp.concatenate([acc[here, HALF:], pltpu.roll(mid, 64, 1)], axis=1)
            cot = held[pl.ds(r, 64), :].astype(jnp.float32)
            sig = 0.5 * jnp.tanh(0.5 * gate) + 0.5
            scaled = cot * sig
            grads[here, :HALF] = (scaled * up_ * (1.0 + gate * (1.0 - sig))).astype(jnp.bfloat16)
            grads[here, HALF:] = (scaled * gate).astype(jnp.bfloat16)

    def finish(n):
        if n == 1:
            for m in range(2):
                landed(hgp.at[:, pl.ds(m * ALIGNED, (ALIGNED, 128)[m])], hg_s.at[m], hg_r.at[m])
        gradients((hgo, hgp)[n], n * ROWS)
        parts[n] = contract_last(proj[...], grads[n * ROWS : (n + 1) * ROWS, :]).astype(jnp.bfloat16)
        for k in range(1 - n, 8):
            j = (t + k) % 8
            rows = pl.ds(pl.multiple_of(j * 16, 16), 16)
            m = 8 * n + k
            send(parts.at[n, rows], arrived.at[m], rs_s.at[m], rs_r.at[m], (pair_dp if n else dp, j))

    seen = set()

    def ring(s, k):
        z_wait(s, k)
        if s == 4:
            sib_send(7 + ORDER.index(k), 4, k)
        elif all(("z", s, other_k) in seen for other_k in range(4)):
            sib_send(2 * s - 1, s)
            sib_send(2 * s, -s)

    def first_hop(k):
        w1_wait(k)
        if all(("w1", other_k) in seen for other_k in (1, 2, 3)):
            sib_send(0, 0)

    def project_inputs():
        in_t[...] = contract_last(inp[...], toks[:ROWS]).astype(jnp.bfloat16)

    actions = {
        "z": ring,
        "w1": first_hop,
        "t1": t1_wait,
        "t2": t2_wait,
        "xn": x_near,
        "xf": x_other,
        "fr": x_far_right,
        "fl": x_far_left,
        "sib": lambda i: sib_wait(i, SIB[i][0], SIB[i][1]),
        "in": project_inputs,
        "mul": product,
        "finish": finish,
    }
    for name, *which in PLAN:
        seen.add((name, *which))
        actions[name](*which)

    side = parts[0, pl.ds(pl.multiple_of(t * 16, 16), 16), :].astype(jnp.float32)
    for k in (*range(8, 16), *range(1, 8)):
        landed(arrived.at[k], rs_s.at[k], rs_r.at[k])
        side += arrived[k].astype(jnp.float32)
    side = side.astype(jnp.bfloat16)

    slot = lax.broadcasted_iota(jnp.int32, (RANK, ROWS), 1)
    held = in_t[...]
    for n in range(2):
        used = (slot >= n * DOC_LEN) & (slot < n * DOC_LEN + len_ref[n])
        features = 0.0625 * contract_last(side, jnp.where(used, held, jnp.zeros_like(held)))
        og_ref[n] = features[:8]
        ou_ref[n] = features[8:]

    for copy in started:
        copy.wait_send()


def shards(tokens, doc_lengths, gate_weight, up_weight, hidden_grad, in_projector, gate_projector, up_projector):
    bf, f32 = jnp.bfloat16, jnp.float32
    dma = pltpu.SemaphoreType.DMA
    out = jax.ShapeDtypeStruct((2, 8, RANK), f32)
    pairs = [26, 3, 3, 16, 16, 16, 16, 11, 11, 3, 3, 3, 3, 9, 9, 9, 9, 2, 2, 16, 16]
    gate_features, up_features = pl.pallas_call(
        kernel,
        out_shape=(out, out),
        in_specs=[pl.BlockSpec(memory_space=pltpu.HBM)] * 8,
        out_specs=(pl.BlockSpec(memory_space=pltpu.VMEM),) * 2,
        scratch_shapes=[
            pltpu.VMEM((2 * ROWS, D), bf),
            pltpu.VMEM((SHARD, COLS), bf),
            pltpu.VMEM((SHARD, COLS), bf),
            pltpu.VMEM((SHARD, COLS), bf),
            pltpu.VMEM((ZS, YS, 2, SHARD, COLS), bf),
            pltpu.VMEM((ROWS, HALF), bf),
            pltpu.VMEM((ROWS, HALF), bf),
            pltpu.VMEM((RANK, D), bf),
            pltpu.VMEM((RANK, HALF), bf),
            pltpu.VMEM((RANK, HALF), bf),
            pltpu.VMEM((2 * ROWS, COLS), f32),
            pltpu.VMEM((2 * ROWS, 2 * HALF), bf),
            pltpu.VMEM((2 * RANK, 2 * HALF), bf),
            pltpu.VMEM((2, 2 * RANK, ROWS), bf),
            pltpu.VMEM((16, 16, ROWS), bf),
            pltpu.VMEM((RANK, ROWS), bf),
            pltpu.SMEM((2,), jnp.int32),
        ]
        + [dma((n,)) for n in pairs],
        compiler_params=pltpu.CompilerParams(
            collective_id=0, has_side_effects=True, vmem_limit_bytes=58 * 2**20
        ),
        name="features",
    )(
        doc_lengths, tokens, gate_weight, up_weight, hidden_grad,
        in_projector, gate_projector, up_projector,
    )
    return gate_features.transpose(0, 2, 1), up_features.transpose(0, 2, 1)


def solution(mesh):
    placed = (
        P("dp", None),
        P("dp"),
        P("dp", "tensor"),
        P("dp", "tensor"),
        P("dp", "tensor"),
        P(),
        P(None, "tensor"),
        P(None, "tensor"),
    )
    return jax.shard_map(
        shards,
        mesh=mesh,
        in_specs=placed,
        out_specs=(P("dp", None, "tensor"), P("dp", None, "tensor")),
        check_vma=False,
    )
```

```python
import jax
import jax.numpy as jnp
from jax import lax
from jax.experimental import pallas as pl
from jax.experimental.pallas import tpu as pltpu
from jax.sharding import PartitionSpec as P

MESH = pl.DeviceIdType.MESH
DOC_LEN = 192
ROWS = 384
D = 4096
COLS = 896
RANK = 64
ALIGNED = 384
HALF = 512
ZS, YS = 8, 4
BLOCK = D // ZS
SHARD = 64
PIECE = 16
SUBS = 3
ORDER = (0, 1, 3, 2)
LAST_RIGHT, LAST_LEFT = (0, 3), (1, 2)
SIB = tuple((dz, None) for dz in (0, 1, -1, 2, -2, 3, -3)) + tuple((4, k) for k in ORDER)
PLAN = (
    ("in",), ("z", 1, 0), ("w1", 1), ("w1", 3), ("t1", 0), ("z", 2, 0), ("w1", 2), ("z", 1, 1), ("sib", 0),
    ("z", 1, 3), ("t2", 0), ("xn", 0), ("t1", 1), ("z", 3, 0), ("z", 1, 2), ("xf", 0), ("sib", 1),
    ("z", 2, 1), ("t2", 1), ("sib", 2), ("fr", 0), ("mul", "own", -1, 1), ("z", 2, 3), ("t1", 2), ("fl", 0),
    ("xn", 1), ("z", 4, 0), ("sib", 7), ("z", 2, 2), ("xf", 1), ("t2", 2), ("sib", 3), ("z", 3, 1),
    ("mul", "own", 2, 2), ("xn", 2), ("sib", 4), ("mul", "own", -2, -2), ("z", 3, 3), ("fr", 1), ("fl", 1),
    ("z", 3, 2), ("z", 4, 1), ("xf", 2), ("sib", 5), ("mul", "own", 3, 3), ("z", 4, 3), ("sib", 6), ("fr", 2),
    ("mul", "own", -3, -3), ("sib", 8), ("sib", 9), ("z", 4, 2), ("sib", 10), ("fl", 2),
    ("mul", "pair", -3, 3), ("mul", "both", 4, 4), ("finish", 1), ("finish", 0),
)
LIMIT = {"zr": 9, "zl": 9, "xr": 9, "xl": 9, "y": 1, "t2": 9}


def contract_last(left, right):
    return lax.dot_general(
        left, right, (((1,), (1,)), ((), ())), preferred_element_type=jnp.float32
    )


def kernel(
    len_hbm, tok_hbm, gw_hbm, uw_hbm, hg_hbm, inp_hbm, gp_hbm, up_hbm,
    og_ref, ou_ref,
    toks, gw, uw, other, w5, hgo, hgp, inp, gp, up,
    acc, grads, proj, parts, arrived, in_t, len_ref,
    loc_sem, w1_s, w1_r, zr_s, zr_r, zl_s, zl_r, sib_s, sib_r,
    t1_s, t1_r, t2_s, t2_r, xr_s, xr_r, xl_s, xl_r, hg_s, hg_r, rs_s, rs_r,
):
    dp, t = lax.axis_index("dp"), lax.axis_index("tensor")
    z, yh, c = dp // 8, (dp // 2) % YS, dp % 2
    yl, x = t // 4, t % 4
    p = yh // 2
    yhp, yhm = YS - 1 - yh, yh + 1 - 2 * (yh % 2)
    origin = (yh, yhm, (yh + 2) % YS, yhp)

    def at(z_, yh_, c_, yl_, x_):
        return (z_ * 8 + yh_ * 2 + c_, yl_ * 4 + x_)

    z_right, z_left = at((z + 1) % ZS, yh, c, yl, x), at((z + ZS - 1) % ZS, yh, c, yl, x)
    sibling = at(z, yh, 1 - c, yl, x)
    pair = at(z, yhp, c, yl, x)
    y_sib = at(z, yh, c, 1 - yl, x)
    x_right, x_left = at(z, yh, c, yl, (x + 1) % 4), at(z, yh, c, yl, (x + 3) % 4)
    pair_dp = pair[0]

    off = pl.multiple_of(p * HALF, 128)
    local = [
        pltpu.make_async_copy(gw_hbm, gw, loc_sem.at[0]),
        pltpu.make_async_copy(uw_hbm, uw, loc_sem.at[1]),
        pltpu.make_async_copy(hg_hbm.at[:, pl.ds(off, ALIGNED)], hgo.at[:, pl.ds(0, ALIGNED)], loc_sem.at[3]),
        pltpu.make_async_copy(hg_hbm.at[:, pl.ds(ALIGNED, 128)], hgo.at[:, pl.ds(ALIGNED, 128)], loc_sem.at[4]),
        pltpu.make_async_copy(gp_hbm.at[:, pl.ds(off, ALIGNED)], gp.at[:, pl.ds(0, ALIGNED)], loc_sem.at[6]),
        pltpu.make_async_copy(gp_hbm.at[:, pl.ds(ALIGNED, 128)], gp.at[:, pl.ds(ALIGNED, 128)], loc_sem.at[7]),
        pltpu.make_async_copy(up_hbm.at[:, pl.ds(off, ALIGNED)], up.at[:, pl.ds(0, ALIGNED)], loc_sem.at[8]),
        pltpu.make_async_copy(up_hbm.at[:, pl.ds(ALIGNED, 128)], up.at[:, pl.ds(ALIGNED, 128)], loc_sem.at[9]),
        pltpu.make_async_copy(len_hbm, len_ref, loc_sem.at[2]),
    ]
    def width(r):
        return pl.ds(pl.multiple_of((z + r + 5) % ZS * BLOCK, BLOCK), BLOCK)

    for r in range(ZS):
        here = pl.ds(r * BLOCK, BLOCK)
        local.append(
            pltpu.make_async_copy(tok_hbm.at[:, width(r)], toks.at[pl.ds(0, ROWS), here], loc_sem.at[10 + r])
        )
    for r in range(ZS):
        here = pl.ds(r * BLOCK, BLOCK)
        local.append(pltpu.make_async_copy(inp_hbm.at[:, width(r)], inp.at[:, here], loc_sem.at[18 + r]))
    for copy in local:
        copy.start()

    barrier = pltpu.get_barrier_semaphore()
    mate = at(z, yhm, c, yl, x)
    greeted = [z_right, z_left, sibling, mate]
    for who in greeted:
        pl.semaphore_signal(barrier, inc=1, device_id=who, device_id_type=MESH)
    for k in range(1, 8):
        pl.semaphore_signal(barrier, inc=1, device_id=(dp, (t + k) % 8), device_id_type=MESH)
    for k in range(8):
        pl.semaphore_signal(barrier, inc=1, device_id=(pair_dp, (t + k) % 8), device_id_type=MESH)

    local[0].wait()
    local[1].wait()
    lane = lax.broadcasted_iota(jnp.int32, (SHARD, 128), 1)
    g3 = gw[:, ALIGNED:HALF].astype(jnp.float32)
    u3 = pltpu.roll(uw[:, ALIGNED:HALF].astype(jnp.float32), 64, 1)
    mid0 = jnp.where(lane < 64, g3, u3).astype(jnp.bfloat16)
    mid1 = jnp.where(lane < 64, u3, g3).astype(jnp.bfloat16)

    def pack(even):
        lo = jnp.concatenate([gw[:, :ALIGNED], mid0, uw[:, :ALIGNED]], axis=1)
        hi = jnp.concatenate([gw[:, HALF:], mid1, uw[:, HALF:]], axis=1)
        return jnp.where(even, lo, hi)

    w5[3, yh, c] = pack(p == 0)
    other[...] = pack(p == 1)

    pl.semaphore_wait(barrier, len(greeted) + 15)

    started = []

    def send(src, dst, ss, rs, who):
        copy = pltpu.make_async_remote_copy(
            src_ref=src, dst_ref=dst, send_sem=ss, recv_sem=rs, device_id=who, device_id_type=MESH
        )
        copy.start()
        started.append(copy)

    flying, queued = dict.fromkeys(LIMIT, 0), {stream: [] for stream in LIMIT}

    def pump(stream):
        while queued[stream] and flying[stream] < LIMIT[stream]:
            flying[stream] += 1
            send(*queued[stream].pop(0))

    def post(stream, *copy):
        queued[stream].append(copy)
        pump(stream)

    def done(*streams):
        for stream in streams:
            flying[stream] -= 1
            pump(stream)

    def landed(dst, ss, rs):
        pltpu.make_async_remote_copy(
            src_ref=dst, dst_ref=dst, send_sem=ss, recv_sem=rs, device_id=sibling, device_id_type=MESH
        ).wait_recv()

    def chunk(dz, k):
        return w5.at[3 + dz, origin[k], c]

    def z_send_right(s, k):
        i = (s - 1) * 4 + k
        post("zr", chunk(1 - s, k), chunk(-s if s < 4 else 4, k), zr_s.at[i], zr_r.at[i], z_right)

    def z_send_left(s, k):
        i = (s - 1) * 4 + k
        post("zl", chunk(s - 1, k), chunk(s, k), zl_s.at[i], zl_r.at[i], z_left)

    def pass_on(s, k):
        if s < 4 or k in LAST_RIGHT:
            z_send_right(s, k)
        if s < 4 or k in LAST_LEFT:
            z_send_left(s, k)

    def z_wait(s, k):
        i = (s - 1) * 4 + k
        if s < 4 or k in LAST_RIGHT:
            landed(chunk(-s if s < 4 else 4, k), zr_s.at[i], zr_r.at[i])
            done("zr")
        if s < 4 or k in LAST_LEFT:
            landed(chunk(s, k), zl_s.at[i], zl_r.at[i])
            done("zl")
        if s < 4:
            pass_on(s + 1, k)

    def sib_send(i, dz, k=None):
        ref = w5.at[3 + dz, :, c] if k is None else chunk(dz, k)
        send(ref, ref, sib_s.at[i], sib_r.at[i], sibling)

    def sib_wait(i, dz, k=None):
        ref = w5.at[3 + dz, :, 1 - c] if k is None else w5.at[3 + dz, origin[k], 1 - c]
        landed(ref, sib_s.at[i], sib_r.at[i])

    def piece(xx, yy, i, base=ROWS):
        start = base + 96 * ((x + xx + 4) % 4) + 48 * yy + PIECE * i
        return pl.ds(pl.multiple_of(start, PIECE), PIECE)

    def t1_send(i):
        post("y", toks.at[piece(0, yl, i, 0)], toks.at[piece(0, yl, i)], t1_s.at[i], t1_r.at[i], pair)

    def x_sends(ref, n):
        post("xr", ref, ref, xr_s.at[n], xr_r.at[n], x_right)
        post("xl", ref, ref, xl_s.at[n], xl_r.at[n], x_left)

    def t1_wait(i):
        ref = toks.at[piece(0, yl, i)]
        landed(ref, t1_s.at[i], t1_r.at[i])
        done("y")
        post("t2", ref, ref, t2_s.at[i], t2_r.at[i], y_sib)
        x_sends(ref, i)
        if i == SUBS - 1:
            send_cotangent()

    def t2_wait(i):
        ref = toks.at[piece(0, 1 - yl, i)]
        landed(ref, t2_s.at[i], t2_r.at[i])
        done("t2")
        x_sends(ref, SUBS + i)

    def x_near(i):
        ref_l, ref_r = toks.at[piece(-1, yl, i)], toks.at[piece(1, yl, i)]
        landed(ref_l, xr_s.at[i], xr_r.at[i])
        landed(ref_r, xl_s.at[i], xl_r.at[i])
        done("xr", "xl")
        m = 2 * SUBS + i
        post("xr", ref_l, ref_l, xr_s.at[m], xr_r.at[m], x_right)

    def x_other(i):
        n = SUBS + i
        ref_l, ref_r = toks.at[piece(-1, 1 - yl, i)], toks.at[piece(1, 1 - yl, i)]
        landed(ref_l, xr_s.at[n], xr_r.at[n])
        landed(ref_r, xl_s.at[n], xl_r.at[n])
        done("xr", "xl")
        m = 2 * SUBS + i
        post("xl", ref_r, ref_r, xl_s.at[m], xl_r.at[m], x_left)

    def x_far_right(i):
        m = 2 * SUBS + i
        landed(toks.at[piece(-2, yl, i)], xr_s.at[m], xr_r.at[m])
        done("xr")

    def x_far_left(i):
        m = 2 * SUBS + i
        landed(toks.at[piece(2, 1 - yl, i)], xl_s.at[m], xl_r.at[m])
        done("xl")

    fresh = [True, True]

    def product(who, a, b):
        lo, hi = {"own": (0, ROWS), "pair": (ROWS, 2 * ROWS), "both": (0, 2 * ROWS)}[who]
        depth = (b - a + 1) * BLOCK
        term = jnp.dot(
            toks[lo:hi, (a + 3) * BLOCK : (b + 4) * BLOCK],
            w5[a + 3 : b + 4].reshape(depth, COLS),
            preferred_element_type=jnp.float32,
        )
        if fresh[lo // ROWS]:
            acc[lo:hi, :] = term
        else:
            acc[lo:hi, :] += term
        for n in range(lo // ROWS, hi // ROWS):
            fresh[n] = False

    pass_on(1, 0)
    for copy in local[2:]:
        copy.wait()
    mine = w5.at[3, yh, c]
    send(other, mine, w1_s.at[2], w1_r.at[2], pair)
    send(mine, mine, w1_s.at[0], w1_r.at[0], mate)
    for i in range(SUBS):
        t1_send(i)

    def send_cotangent():
        off_pair = pl.multiple_of((1 - p) * HALF, 128)
        send(hg_hbm.at[:, pl.ds(off_pair, ALIGNED)], hgp.at[:, pl.ds(0, ALIGNED)], hg_s.at[0], hg_r.at[0], pair)
        send(hg_hbm.at[:, pl.ds(ALIGNED, 128)], hgp.at[:, pl.ds(ALIGNED, 128)], hg_s.at[1], hg_r.at[1], pair)

    def w1_wait(k):
        ref = chunk(0, k)
        landed(ref, w1_s.at[k - 1], w1_r.at[k - 1])
        if k == 3:
            send(ref, ref, w1_s.at[1], w1_r.at[1], mate)
        pass_on(1, k)

    side_lane = lax.broadcasted_iota(jnp.int32, (RANK, HALF), 1)
    valid = (side_lane < ALIGNED) | ((side_lane < ALIGNED + 64) == (p == 0))
    g_rows = jnp.where(valid, gp[...].astype(jnp.float32), 0.0).reshape(8, 8, HALF)
    u_rows = jnp.where(valid, up[...].astype(jnp.float32), 0.0).reshape(8, 8, HALF)
    none = jnp.zeros_like(g_rows)
    proj[...] = jnp.concatenate(
        [jnp.concatenate([g_rows, none], axis=2), jnp.concatenate([none, u_rows], axis=2)], axis=1
    ).reshape(2 * RANK, 2 * HALF).astype(jnp.bfloat16)

    def gradients(held, row):
        @pl.loop(0, ROWS // 64)
        def _(j):
            r = pl.multiple_of(j * 64, 64)
            here = pl.ds(row + r, 64)
            mid = acc[here, ALIGNED:HALF]
            gate = jnp.concatenate([acc[here, :ALIGNED], mid], axis=1)
            up_ = jnp.concatenate([acc[here, HALF:], pltpu.roll(mid, 64, 1)], axis=1)
            cot = held[pl.ds(r, 64), :].astype(jnp.float32)
            sig = 0.5 * jnp.tanh(0.5 * gate) + 0.5
            scaled = cot * sig
            grads[here, :HALF] = (scaled * up_ * (1.0 + gate * (1.0 - sig))).astype(jnp.bfloat16)
            grads[here, HALF:] = (scaled * gate).astype(jnp.bfloat16)

    def finish(n):
        if n == 1:
            for m in range(2):
                landed(hgp.at[:, pl.ds(m * ALIGNED, (ALIGNED, 128)[m])], hg_s.at[m], hg_r.at[m])
        gradients((hgo, hgp)[n], n * ROWS)
        parts[n] = contract_last(proj[...], grads[n * ROWS : (n + 1) * ROWS, :]).astype(jnp.bfloat16)
        for k in range(1 - n, 8):
            j = (t + k) % 8
            rows = pl.ds(pl.multiple_of(j * 16, 16), 16)
            m = 8 * n + k
            send(parts.at[n, rows], arrived.at[m], rs_s.at[m], rs_r.at[m], (pair_dp if n else dp, j))

    seen = set()

    def ring(s, k):
        z_wait(s, k)
        if s == 4:
            sib_send(7 + ORDER.index(k), 4, k)
        elif all(("z", s, other_k) in seen for other_k in range(4)):
            sib_send(2 * s - 1, s)
            sib_send(2 * s, -s)

    def first_hop(k):
        w1_wait(k)
        if all(("w1", other_k) in seen for other_k in (1, 2, 3)):
            sib_send(0, 0)

    def project_inputs():
        in_t[...] = contract_last(inp[...], toks[:ROWS]).astype(jnp.bfloat16)

    actions = {
        "z": ring,
        "w1": first_hop,
        "t1": t1_wait,
        "t2": t2_wait,
        "xn": x_near,
        "xf": x_other,
        "fr": x_far_right,
        "fl": x_far_left,
        "sib": lambda i: sib_wait(i, SIB[i][0], SIB[i][1]),
        "in": project_inputs,
        "mul": product,
        "finish": finish,
    }
    for name, *which in PLAN:
        seen.add((name, *which))
        actions[name](*which)

    side = parts[0, pl.ds(pl.multiple_of(t * 16, 16), 16), :].astype(jnp.float32)
    for k in (*range(8, 16), *range(1, 8)):
        landed(arrived.at[k], rs_s.at[k], rs_r.at[k])
        side += arrived[k].astype(jnp.float32)
    side = side.astype(jnp.bfloat16)

    slot = lax.broadcasted_iota(jnp.int32, (RANK, ROWS), 1)
    held = in_t[...]
    for n in range(2):
        used = (slot >= n * DOC_LEN) & (slot < n * DOC_LEN + len_ref[n])
        features = 0.0625 * contract_last(side, jnp.where(used, held, jnp.zeros_like(held)))
        og_ref[n] = features[:8]
        ou_ref[n] = features[8:]

    for copy in started:
        copy.wait_send()


def shards(tokens, doc_lengths, gate_weight, up_weight, hidden_grad, in_projector, gate_projector, up_projector):
    bf, f32 = jnp.bfloat16, jnp.float32
    dma = pltpu.SemaphoreType.DMA
    out = jax.ShapeDtypeStruct((2, 8, RANK), f32)
    pairs = [26, 3, 3, 16, 16, 16, 16, 11, 11, 3, 3, 3, 3, 9, 9, 9, 9, 2, 2, 16, 16]
    gate_features, up_features = pl.pallas_call(
        kernel,
        out_shape=(out, out),
        in_specs=[pl.BlockSpec(memory_space=pltpu.HBM)] * 8,
        out_specs=(pl.BlockSpec(memory_space=pltpu.VMEM),) * 2,
        scratch_shapes=[
            pltpu.VMEM((2 * ROWS, D), bf),
            pltpu.VMEM((SHARD, COLS), bf),
            pltpu.VMEM((SHARD, COLS), bf),
            pltpu.VMEM((SHARD, COLS), bf),
            pltpu.VMEM((ZS, YS, 2, SHARD, COLS), bf),
            pltpu.VMEM((ROWS, HALF), bf),
            pltpu.VMEM((ROWS, HALF), bf),
            pltpu.VMEM((RANK, D), bf),
            pltpu.VMEM((RANK, HALF), bf),
            pltpu.VMEM((RANK, HALF), bf),
            pltpu.VMEM((2 * ROWS, COLS), f32),
            pltpu.VMEM((2 * ROWS, 2 * HALF), bf),
            pltpu.VMEM((2 * RANK, 2 * HALF), bf),
            pltpu.VMEM((2, 2 * RANK, ROWS), bf),
            pltpu.VMEM((16, 16, ROWS), bf),
            pltpu.VMEM((RANK, ROWS), bf),
            pltpu.SMEM((2,), jnp.int32),
        ]
        + [dma((n,)) for n in pairs],
        compiler_params=pltpu.CompilerParams(
            collective_id=0, has_side_effects=True, vmem_limit_bytes=58 * 2**20
        ),
        name="features",
    )(
        doc_lengths, tokens, gate_weight, up_weight, hidden_grad,
        in_projector, gate_projector, up_projector,
    )
    return gate_features.transpose(0, 2, 1), up_features.transpose(0, 2, 1)


def solution(mesh):
    placed = (
        P("dp", None),
        P("dp"),
        P("dp", "tensor"),
        P("dp", "tensor"),
        P("dp", "tensor"),
        P(),
        P(None, "tensor"),
        P(None, "tensor"),
    )
    return jax.shard_map(
        shards,
        mesh=mesh,
        in_specs=placed,
        out_specs=(P("dp", None, "tensor"), P("dp", None, "tensor")),
        check_vma=False,
    )
```

```python
import jax
import jax.numpy as jnp
from jax import lax
from jax.experimental import pallas as pl
from jax.experimental.pallas import tpu as pltpu
from jax.sharding import PartitionSpec as P

MESH = pl.DeviceIdType.MESH
DOC_LEN = 192
ROWS = 384
D = 4096
COLS = 896
RANK = 64
ALIGNED = 384
HALF = 512
ZS, YS = 8, 4
BLOCK = D // ZS
SHARD = 64
PIECE = 16
SUBS = 3
ORDER = (0, 1, 3, 2)
LAST_RIGHT, LAST_LEFT = (0, 3), (1, 2)
SIB = tuple((dz, None) for dz in (0, 1, -1, 2, -2, 3, -3)) + tuple((4, k) for k in ORDER)
PLAN = (
    ("in",), ("z", 1, 0), ("w1", 1), ("w1", 3), ("t1", 0), ("z", 2, 0), ("w1", 2), ("z", 1, 1), ("sib", 0),
    ("z", 1, 3), ("t2", 0), ("xn", 0), ("t1", 1), ("z", 3, 0), ("z", 1, 2), ("xf", 0), ("sib", 1),
    ("z", 2, 1), ("t2", 1), ("sib", 2), ("fr", 0), ("mul", "own", -1, 1), ("z", 2, 3), ("t1", 2), ("fl", 0),
    ("xn", 1), ("z", 4, 0), ("sib", 7), ("z", 2, 2), ("xf", 1), ("t2", 2), ("sib", 3), ("z", 3, 1),
    ("mul", "own", 2, 2), ("xn", 2), ("sib", 4), ("mul", "own", -2, -2), ("z", 3, 3), ("fr", 1), ("fl", 1),
    ("z", 3, 2), ("z", 4, 1), ("xf", 2), ("sib", 5), ("mul", "own", 3, 3), ("z", 4, 3), ("sib", 6), ("fr", 2),
    ("mul", "own", -3, -3), ("sib", 8), ("sib", 9), ("z", 4, 2), ("sib", 10), ("fl", 2),
    ("mul", "pair", -3, 3), ("mul", "both", 4, 4), ("finish", 1), ("finish", 0),
)
LIMIT = {"zr": 9, "zl": 9, "xr": 9, "xl": 9, "y": 1, "t2": 9}


def contract_last(left, right):
    return lax.dot_general(
        left, right, (((1,), (1,)), ((), ())), preferred_element_type=jnp.float32
    )


def kernel(
    len_hbm, tok_hbm, gw_hbm, uw_hbm, hg_hbm, inp_hbm, gp_hbm, up_hbm,
    og_ref, ou_ref,
    toks, gw, uw, other, w5, hgo, hgp, inp, gp, up,
    acc, grads, proj, parts, arrived, in_t, len_ref,
    loc_sem, w1_s, w1_r, zr_s, zr_r, zl_s, zl_r, sib_s, sib_r,
    t1_s, t1_r, t2_s, t2_r, xr_s, xr_r, xl_s, xl_r, hg_s, hg_r, rs_s, rs_r,
):
    dp, t = lax.axis_index("dp"), lax.axis_index("tensor")
    z, yh, c = dp // 8, (dp // 2) % YS, dp % 2
    yl, x = t // 4, t % 4
    p = yh // 2
    yhp, yhm = YS - 1 - yh, yh + 1 - 2 * (yh % 2)
    origin = (yh, yhm, (yh + 2) % YS, yhp)

    def at(z_, yh_, c_, yl_, x_):
        return (z_ * 8 + yh_ * 2 + c_, yl_ * 4 + x_)

    z_right, z_left = at((z + 1) % ZS, yh, c, yl, x), at((z + ZS - 1) % ZS, yh, c, yl, x)
    sibling = at(z, yh, 1 - c, yl, x)
    pair = at(z, yhp, c, yl, x)
    y_sib = at(z, yh, c, 1 - yl, x)
    x_right, x_left = at(z, yh, c, yl, (x + 1) % 4), at(z, yh, c, yl, (x + 3) % 4)
    pair_dp = pair[0]

    barrier = pltpu.get_barrier_semaphore()
    mate = at(z, yhm, c, yl, x)
    greeted = [z_right, z_left, sibling, mate]
    for who in greeted:
        pl.semaphore_signal(barrier, inc=1, device_id=who, device_id_type=MESH)
    for k in range(1, 8):
        pl.semaphore_signal(barrier, inc=1, device_id=(dp, (t + k) % 8), device_id_type=MESH)
    for k in range(8):
        pl.semaphore_signal(barrier, inc=1, device_id=(pair_dp, (t + k) % 8), device_id_type=MESH)

    off = pl.multiple_of(p * HALF, 128)
    local = [
        pltpu.make_async_copy(gw_hbm, gw, loc_sem.at[0]),
        pltpu.make_async_copy(uw_hbm, uw, loc_sem.at[1]),
        pltpu.make_async_copy(hg_hbm.at[:, pl.ds(off, ALIGNED)], hgo.at[:, pl.ds(0, ALIGNED)], loc_sem.at[3]),
        pltpu.make_async_copy(hg_hbm.at[:, pl.ds(ALIGNED, 128)], hgo.at[:, pl.ds(ALIGNED, 128)], loc_sem.at[4]),
        pltpu.make_async_copy(gp_hbm.at[:, pl.ds(off, ALIGNED)], gp.at[:, pl.ds(0, ALIGNED)], loc_sem.at[6]),
        pltpu.make_async_copy(gp_hbm.at[:, pl.ds(ALIGNED, 128)], gp.at[:, pl.ds(ALIGNED, 128)], loc_sem.at[7]),
        pltpu.make_async_copy(up_hbm.at[:, pl.ds(off, ALIGNED)], up.at[:, pl.ds(0, ALIGNED)], loc_sem.at[8]),
        pltpu.make_async_copy(up_hbm.at[:, pl.ds(ALIGNED, 128)], up.at[:, pl.ds(ALIGNED, 128)], loc_sem.at[9]),
        pltpu.make_async_copy(len_hbm, len_ref, loc_sem.at[2]),
    ]
    def width(r):
        return pl.ds(pl.multiple_of((z + r + 5) % ZS * BLOCK, BLOCK), BLOCK)

    for r in range(ZS):
        here = pl.ds(r * BLOCK, BLOCK)
        local.append(
            pltpu.make_async_copy(tok_hbm.at[:, width(r)], toks.at[pl.ds(0, ROWS), here], loc_sem.at[10 + r])
        )
    for r in range(ZS):
        here = pl.ds(r * BLOCK, BLOCK)
        local.append(pltpu.make_async_copy(inp_hbm.at[:, width(r)], inp.at[:, here], loc_sem.at[18 + r]))
    for copy in local[:2] + local[9:17] + local[2:9] + local[17:]:
        copy.start()

    local[0].wait()
    local[1].wait()
    lane = lax.broadcasted_iota(jnp.int32, (SHARD, 128), 1)
    g3 = gw[:, ALIGNED:HALF].astype(jnp.float32)
    u3 = pltpu.roll(uw[:, ALIGNED:HALF].astype(jnp.float32), 64, 1)
    mid0 = jnp.where(lane < 64, g3, u3).astype(jnp.bfloat16)
    mid1 = jnp.where(lane < 64, u3, g3).astype(jnp.bfloat16)

    def pack(even):
        lo = jnp.concatenate([gw[:, :ALIGNED], mid0, uw[:, :ALIGNED]], axis=1)
        hi = jnp.concatenate([gw[:, HALF:], mid1, uw[:, HALF:]], axis=1)
        return jnp.where(even, lo, hi)

    w5[3, yh, c] = pack(p == 0)
    other[...] = pack(p == 1)

    pl.semaphore_wait(barrier, len(greeted) + 15)

    started = []

    def send(src, dst, ss, rs, who):
        copy = pltpu.make_async_remote_copy(
            src_ref=src, dst_ref=dst, send_sem=ss, recv_sem=rs, device_id=who, device_id_type=MESH
        )
        copy.start()
        started.append(copy)

    flying, queued = dict.fromkeys(LIMIT, 0), {stream: [] for stream in LIMIT}

    def pump(stream):
        while queued[stream] and flying[stream] < LIMIT[stream]:
            flying[stream] += 1
            send(*queued[stream].pop(0))

    def post(stream, *copy):
        queued[stream].append(copy)
        pump(stream)

    def done(*streams):
        for stream in streams:
            flying[stream] -= 1
            pump(stream)

    def landed(dst, ss, rs):
        pltpu.make_async_remote_copy(
            src_ref=dst, dst_ref=dst, send_sem=ss, recv_sem=rs, device_id=sibling, device_id_type=MESH
        ).wait_recv()

    def chunk(dz, k):
        return w5.at[3 + dz, origin[k], c]

    def z_send_right(s, k):
        i = (s - 1) * 4 + k
        post("zr", chunk(1 - s, k), chunk(-s if s < 4 else 4, k), zr_s.at[i], zr_r.at[i], z_right)

    def z_send_left(s, k):
        i = (s - 1) * 4 + k
        post("zl", chunk(s - 1, k), chunk(s, k), zl_s.at[i], zl_r.at[i], z_left)

    def pass_on(s, k):
        if s < 4 or k in LAST_RIGHT:
            z_send_right(s, k)
        if s < 4 or k in LAST_LEFT:
            z_send_left(s, k)

    def z_wait(s, k):
        i = (s - 1) * 4 + k
        if s < 4 or k in LAST_RIGHT:
            landed(chunk(-s if s < 4 else 4, k), zr_s.at[i], zr_r.at[i])
            done("zr")
        if s < 4 or k in LAST_LEFT:
            landed(chunk(s, k), zl_s.at[i], zl_r.at[i])
            done("zl")
        if s < 4:
            pass_on(s + 1, k)

    def sib_send(i, dz, k=None):
        ref = w5.at[3 + dz, :, c] if k is None else chunk(dz, k)
        send(ref, ref, sib_s.at[i], sib_r.at[i], sibling)

    def sib_wait(i, dz, k=None):
        ref = w5.at[3 + dz, :, 1 - c] if k is None else w5.at[3 + dz, origin[k], 1 - c]
        landed(ref, sib_s.at[i], sib_r.at[i])

    def piece(xx, yy, i, base=ROWS):
        start = base + 96 * ((x + xx + 4) % 4) + 48 * yy + PIECE * i
        return pl.ds(pl.multiple_of(start, PIECE), PIECE)

    def t1_send(i):
        post("y", toks.at[piece(0, yl, i, 0)], toks.at[piece(0, yl, i)], t1_s.at[i], t1_r.at[i], pair)

    def x_sends(ref, n):
        post("xr", ref, ref, xr_s.at[n], xr_r.at[n], x_right)
        post("xl", ref, ref, xl_s.at[n], xl_r.at[n], x_left)

    def t1_wait(i):
        ref = toks.at[piece(0, yl, i)]
        landed(ref, t1_s.at[i], t1_r.at[i])
        done("y")
        post("t2", ref, ref, t2_s.at[i], t2_r.at[i], y_sib)
        x_sends(ref, i)
        if i == SUBS - 1:
            send_cotangent()

    def t2_wait(i):
        ref = toks.at[piece(0, 1 - yl, i)]
        landed(ref, t2_s.at[i], t2_r.at[i])
        done("t2")
        x_sends(ref, SUBS + i)

    def x_near(i):
        ref_l, ref_r = toks.at[piece(-1, yl, i)], toks.at[piece(1, yl, i)]
        landed(ref_l, xr_s.at[i], xr_r.at[i])
        landed(ref_r, xl_s.at[i], xl_r.at[i])
        done("xr", "xl")
        m = 2 * SUBS + i
        post("xr", ref_l, ref_l, xr_s.at[m], xr_r.at[m], x_right)

    def x_other(i):
        n = SUBS + i
        ref_l, ref_r = toks.at[piece(-1, 1 - yl, i)], toks.at[piece(1, 1 - yl, i)]
        landed(ref_l, xr_s.at[n], xr_r.at[n])
        landed(ref_r, xl_s.at[n], xl_r.at[n])
        done("xr", "xl")
        m = 2 * SUBS + i
        post("xl", ref_r, ref_r, xl_s.at[m], xl_r.at[m], x_left)

    def x_far_right(i):
        m = 2 * SUBS + i
        landed(toks.at[piece(-2, yl, i)], xr_s.at[m], xr_r.at[m])
        done("xr")

    def x_far_left(i):
        m = 2 * SUBS + i
        landed(toks.at[piece(2, 1 - yl, i)], xl_s.at[m], xl_r.at[m])
        done("xl")

    fresh = [True, True]

    def product(who, a, b):
        lo, hi = {"own": (0, ROWS), "pair": (ROWS, 2 * ROWS), "both": (0, 2 * ROWS)}[who]
        depth = (b - a + 1) * BLOCK
        term = jnp.dot(
            toks[lo:hi, (a + 3) * BLOCK : (b + 4) * BLOCK],
            w5[a + 3 : b + 4].reshape(depth, COLS),
            preferred_element_type=jnp.float32,
        )
        if fresh[lo // ROWS]:
            acc[lo:hi, :] = term
        else:
            acc[lo:hi, :] += term
        for n in range(lo // ROWS, hi // ROWS):
            fresh[n] = False

    pass_on(1, 0)
    mine = w5.at[3, yh, c]
    send(other, mine, w1_s.at[2], w1_r.at[2], pair)
    send(mine, mine, w1_s.at[0], w1_r.at[0], mate)
    for copy in local[9:17]:
        copy.wait()
    for i in range(SUBS):
        t1_send(i)

    def send_cotangent():
        off_pair = pl.multiple_of((1 - p) * HALF, 128)
        send(hg_hbm.at[:, pl.ds(off_pair, ALIGNED)], hgp.at[:, pl.ds(0, ALIGNED)], hg_s.at[0], hg_r.at[0], pair)
        send(hg_hbm.at[:, pl.ds(ALIGNED, 128)], hgp.at[:, pl.ds(ALIGNED, 128)], hg_s.at[1], hg_r.at[1], pair)

    def w1_wait(k):
        ref = chunk(0, k)
        landed(ref, w1_s.at[k - 1], w1_r.at[k - 1])
        if k == 3:
            send(ref, ref, w1_s.at[1], w1_r.at[1], mate)
        pass_on(1, k)

    for copy in local[2:9] + local[17:]:
        copy.wait()
    side_lane = lax.broadcasted_iota(jnp.int32, (RANK, HALF), 1)
    valid = (side_lane < ALIGNED) | ((side_lane < ALIGNED + 64) == (p == 0))
    g_rows = jnp.where(valid, gp[...].astype(jnp.float32), 0.0).reshape(8, 8, HALF)
    u_rows = jnp.where(valid, up[...].astype(jnp.float32), 0.0).reshape(8, 8, HALF)
    none = jnp.zeros_like(g_rows)
    proj[...] = jnp.concatenate(
        [jnp.concatenate([g_rows, none], axis=2), jnp.concatenate([none, u_rows], axis=2)], axis=1
    ).reshape(2 * RANK, 2 * HALF).astype(jnp.bfloat16)

    def gradients(held, row):
        @pl.loop(0, ROWS // 64)
        def _(j):
            r = pl.multiple_of(j * 64, 64)
            here = pl.ds(row + r, 64)
            mid = acc[here, ALIGNED:HALF]
            gate = jnp.concatenate([acc[here, :ALIGNED], mid], axis=1)
            up_ = jnp.concatenate([acc[here, HALF:], pltpu.roll(mid, 64, 1)], axis=1)
            cot = held[pl.ds(r, 64), :].astype(jnp.float32)
            sig = 0.5 * jnp.tanh(0.5 * gate) + 0.5
            scaled = cot * sig
            grads[here, :HALF] = (scaled * up_ * (1.0 + gate * (1.0 - sig))).astype(jnp.bfloat16)
            grads[here, HALF:] = (scaled * gate).astype(jnp.bfloat16)

    def finish(n):
        if n == 1:
            for m in range(2):
                landed(hgp.at[:, pl.ds(m * ALIGNED, (ALIGNED, 128)[m])], hg_s.at[m], hg_r.at[m])
        gradients((hgo, hgp)[n], n * ROWS)
        parts[n] = contract_last(proj[...], grads[n * ROWS : (n + 1) * ROWS, :]).astype(jnp.bfloat16)
        for k in range(1 - n, 8):
            j = (t + k) % 8
            rows = pl.ds(pl.multiple_of(j * 16, 16), 16)
            m = 8 * n + k
            send(parts.at[n, rows], arrived.at[m], rs_s.at[m], rs_r.at[m], (pair_dp if n else dp, j))

    seen = set()

    def ring(s, k):
        z_wait(s, k)
        if s == 4:
            sib_send(7 + ORDER.index(k), 4, k)
        elif all(("z", s, other_k) in seen for other_k in range(4)):
            sib_send(2 * s - 1, s)
            sib_send(2 * s, -s)

    def first_hop(k):
        w1_wait(k)
        if all(("w1", other_k) in seen for other_k in (1, 2, 3)):
            sib_send(0, 0)

    def project_inputs():
        in_t[...] = contract_last(inp[...], toks[:ROWS]).astype(jnp.bfloat16)

    actions = {
        "z": ring,
        "w1": first_hop,
        "t1": t1_wait,
        "t2": t2_wait,
        "xn": x_near,
        "xf": x_other,
        "fr": x_far_right,
        "fl": x_far_left,
        "sib": lambda i: sib_wait(i, SIB[i][0], SIB[i][1]),
        "in": project_inputs,
        "mul": product,
        "finish": finish,
    }
    for name, *which in PLAN:
        seen.add((name, *which))
        actions[name](*which)

    side = parts[0, pl.ds(pl.multiple_of(t * 16, 16), 16), :].astype(jnp.float32)
    for k in (*range(8, 16), *range(1, 8)):
        landed(arrived.at[k], rs_s.at[k], rs_r.at[k])
        side += arrived[k].astype(jnp.float32)
    side = side.astype(jnp.bfloat16)

    slot = lax.broadcasted_iota(jnp.int32, (RANK, ROWS), 1)
    held = in_t[...]
    for n in range(2):
        used = (slot >= n * DOC_LEN) & (slot < n * DOC_LEN + len_ref[n])
        features = 0.0625 * contract_last(side, jnp.where(used, held, jnp.zeros_like(held)))
        og_ref[n] = features[:8]
        ou_ref[n] = features[8:]

    for copy in started:
        copy.wait_send()


def shards(tokens, doc_lengths, gate_weight, up_weight, hidden_grad, in_projector, gate_projector, up_projector):
    bf, f32 = jnp.bfloat16, jnp.float32
    dma = pltpu.SemaphoreType.DMA
    out = jax.ShapeDtypeStruct((2, 8, RANK), f32)
    pairs = [26, 3, 3, 16, 16, 16, 16, 11, 11, 3, 3, 3, 3, 9, 9, 9, 9, 2, 2, 16, 16]
    gate_features, up_features = pl.pallas_call(
        kernel,
        out_shape=(out, out),
        in_specs=[pl.BlockSpec(memory_space=pltpu.HBM)] * 8,
        out_specs=(pl.BlockSpec(memory_space=pltpu.VMEM),) * 2,
        scratch_shapes=[
            pltpu.VMEM((2 * ROWS, D), bf),
            pltpu.VMEM((SHARD, COLS), bf),
            pltpu.VMEM((SHARD, COLS), bf),
            pltpu.VMEM((SHARD, COLS), bf),
            pltpu.VMEM((ZS, YS, 2, SHARD, COLS), bf),
            pltpu.VMEM((ROWS, HALF), bf),
            pltpu.VMEM((ROWS, HALF), bf),
            pltpu.VMEM((RANK, D), bf),
            pltpu.VMEM((RANK, HALF), bf),
            pltpu.VMEM((RANK, HALF), bf),
            pltpu.VMEM((2 * ROWS, COLS), f32),
            pltpu.VMEM((2 * ROWS, 2 * HALF), bf),
            pltpu.VMEM((2 * RANK, 2 * HALF), bf),
            pltpu.VMEM((2, 2 * RANK, ROWS), bf),
            pltpu.VMEM((16, 16, ROWS), bf),
            pltpu.VMEM((RANK, ROWS), bf),
            pltpu.SMEM((2,), jnp.int32),
        ]
        + [dma((n,)) for n in pairs],
        compiler_params=pltpu.CompilerParams(
            collective_id=0, has_side_effects=True, vmem_limit_bytes=58 * 2**20
        ),
        name="features",
    )(
        doc_lengths, tokens, gate_weight, up_weight, hidden_grad,
        in_projector, gate_projector, up_projector,
    )
    return gate_features.transpose(0, 2, 1), up_features.transpose(0, 2, 1)


def solution(mesh):
    placed = (
        P("dp", None),
        P("dp"),
        P("dp", "tensor"),
        P("dp", "tensor"),
        P("dp", "tensor"),
        P(),
        P(None, "tensor"),
        P(None, "tensor"),
    )
    return jax.shard_map(
        shards,
        mesh=mesh,
        in_specs=placed,
        out_specs=(P("dp", None, "tensor"), P("dp", None, "tensor")),
        check_vma=False,
    )
```
